32 devices in a mesh: gy: 4 (over y, core), gx: 8 (over z, x).
Axes of the slice: x: 2, y: 2, z: 4, core: 2. Of those that a mesh axis runs over, the one named last changes fastest.
Arguments:
- first_frame: float32 [128, 256, 128], P('gy', 'gx'), may hold values from -6 to 6
- second_frame: float32 [128, 256, 128], P('gy', 'gx'), may hold values from -6 to 6
- source_column: int32 [4, 8, 4, 1], P('gy', 'gx'), may hold values from 0 to 7; in each aligned block of 4 rows (0 to 3, 4 to 7, ..., all dimensions but the last counted through in order) at most 2 rows name the same one
Outputs:
- flow_field: float32 [3, 128, 256, 128], P(None, 'gy', 'gx')
The draws below stay inside these ranges and needn't reach their ends.
Inputs may be any that keep to these rules, and one draw needn't show every extreme that they name: `source_column`: among the 4 bricks of one device at most 2 take the same source column, and in every draw some device has 2 that do.
All inputs are finite; a program needn't handle non-finite values.
Results may differ from the reference program's by a relative error of at most 0.0001.
Values sent between devices are 32-bit elements; how exact they have to be, the bound alone decides.
A program may use at most 384 MiB of HBM per device.

```python
import math
import jax
import jax.numpy as jnp
import numpy as np
from jax import lax

BRICK = 32
CAP = 2
LEVELS = 4
SWEEPS = 2
CYCLES = 1
BCY = 1
BCX = 1
BCZ = 4
BRICKS_DEV = 4
NBX = 8
NY = 128
NX = 256
NZ = 128
N_GY = 4
N_GX = 8


def level_of(stream_key, dims, cuts, low, top_value):
    level, own = 1.0, jax.random.fold_in(stream_key, 6)
    for dim, blocks in cuts:
        steps = jnp.exp(jax.random.uniform(jax.random.fold_in(own, dim), (blocks,), jnp.float32, low / len(cuts), top_value / len(cuts)))
        level = level * jnp.repeat(steps, dims[dim] // blocks).reshape([-1 if axis == dim else 1 for axis in range(len(dims))])
    return level


def shared_out(rng, own, number, rows, amount, top, reach, slope):
    sequence = jax.random.permutation(rng, amount)
    packed, usual = portions_of(amount, rows * top, reach, slope, True), portions_of(amount, rows * top, reach, slope, False)
    places = jnp.arange(amount)

    def named(tallies, rotation):
        used = int((tallies > 0).sum())
        fixed = max(1, used // 4)
        shifted = fixed + (places - fixed + rotation * (used - fixed)) % max(1, amount - fixed)
        return jnp.zeros((amount,), jnp.int32).at[sequence[jnp.where(places < fixed, places, shifted)]].set(jnp.asarray(tallies, jnp.int32))

    tallies = jnp.where(number % 4 == 0, named(packed, number // 4), named(usual, number - number // 4 - 1))
    mixed = jax.random.permutation(jax.random.fold_in(own, 3), amount)
    donor, taker = mixed[0:amount // 2 * 2:2], mixed[1:amount // 2 * 2:2]
    room = jnp.minimum(tallies[donor] - 1, reach - tallies[taker]) // 2
    room = jnp.where((donor == sequence[0]) | (taker == sequence[0]) | (tallies[taker] == 0), 0, jnp.maximum(room, 0))
    shifted = jax.random.randint(jax.random.fold_in(own, 4), (amount // 2,), 0, 1 << 20) % (room + 1)
    tallies = tallies.at[donor].add(-shifted).at[taker].add(shifted)
    members = jnp.searchsorted(jnp.cumsum(tallies), jnp.arange(rows * top), side="right").astype(jnp.int32)
    grid = members.reshape(top, rows).T
    grid = grid[jax.random.permutation(jax.random.fold_in(own, 1), rows)]
    rotation = jax.random.randint(jax.random.fold_in(own, 2), (rows, 1), 0, top)
    return jnp.take_along_axis(grid, (jnp.arange(top)[None, :] + rotation) % top, axis=1)


def portions_of(count, total, most, skew, full):
    loads = [(1 << 20) // math.isqrt(rank ** skew) + 1 for rank in range(1, count + 1)]
    largest = most if full else min(most, max(-(-total // count), total * loads[0] // sum(loads)))
    least = 1 if total - largest >= count - 1 else 0
    given, rest = [largest] + [least] * (count - 1), total - largest - least * (count - 1)
    while rest > 0:
        movable = [i for i in range(1, count) if given[i] < largest] or [i for i in range(1, count) if given[i] < most]
        pool, remaining = sum([loads[i] for i in movable]), rest
        for i in movable:
            extra = min(most - given[i], max(1, remaining * loads[i] // pool), rest)
            given[i] = given[i] + extra
            rest = rest - extra
    return np.array(given)


def normal_values(stream_key, dims, width, reach, split=(), kind=jnp.bfloat16):
    factor_of = level_of(stream_key, dims, split, -0.22, 0.18) if split else 1.0
    array = jax.random.normal(stream_key, dims, jnp.float32) * width * factor_of
    return jnp.minimum(jnp.maximum(array, -reach), reach).astype(kind)


def setup_inputs(seed: int = 0) -> dict:
    seeds = jax.random.split(jax.random.key(seed), 4)
    first_frame = normal_values(seeds[0], (NY, NX, NZ), 1.0, 6.0, ((0, 4), (1, 8)), jnp.float32)
    second_frame = normal_values(seeds[1], (NY, NX, NZ), 1.0, 6.0, ((0, 4), (1, 8)), jnp.float32)
    source_column_keys = jax.random.split(jax.random.fold_in(seeds[2], 1), N_GY * N_GX * BRICKS_DEV // BRICKS_DEV)
    source_column_turns = jax.random.permutation(jax.random.fold_in(seeds[2], 3), N_GY * N_GX * BRICKS_DEV // BRICKS_DEV)
    source_column = jax.vmap(lambda own, number: shared_out(jax.random.fold_in(seeds[2], 2), own, number, BRICKS_DEV, NBX, 1, CAP, 2))(source_column_keys, source_column_turns).reshape((N_GY, N_GX, BRICKS_DEV, 1))
    return dict(first_frame=first_frame, second_frame=second_frame, source_column=source_column)


smoothness = 1.0
tikhonov = 0.05
contrast = 0.5
relaxation = 0.8
gradient_floor = 1.0

def difference(volume, along):
    length = volume.shape[along]
    upper_part = lax.slice_in_dim(volume, 2, length, axis=along)
    lower_part = lax.slice_in_dim(volume, 0, length - 2, axis=along)
    return 0.5 * (upper_part - lower_part)

def smoothen(volume, along):
    length = volume.shape[along]
    lower_part = lax.slice_in_dim(volume, 0, length - 2, axis=along)
    middle = lax.slice_in_dim(volume, 1, length - 1, axis=along)
    upper_part = lax.slice_in_dim(volume, 2, length, axis=along)
    return 0.25 * (lower_part + 2.0 * middle + upper_part)

def motion_terms(padded_mean, temporal):
    grad_rows = smoothen(smoothen(difference(padded_mean, 0), 1), 2)
    grad_cols = smoothen(smoothen(difference(padded_mean, 1), 0), 2)
    grad_planes = smoothen(smoothen(difference(padded_mean, 2), 0), 1)
    normal = 1.0 / (grad_rows * grad_rows + grad_cols * grad_cols + grad_planes * grad_planes + gradient_floor)
    tensor = jnp.stack([grad_rows * grad_rows, grad_rows * grad_cols, grad_rows * grad_planes, grad_cols * grad_cols, grad_cols * grad_planes, grad_planes * grad_planes]) * normal
    source = -jnp.stack([grad_rows * temporal, grad_cols * temporal, grad_planes * temporal]) * normal
    return (tensor, source)

def boundary_masks(row_index, row_count, col_index, col_count, plane_index, plane_count):
    return ((row_index > 0).astype(jnp.float32)[:, None, None], (row_index < row_count - 1).astype(jnp.float32)[:, None, None], (col_index > 0).astype(jnp.float32)[None, :, None], (col_index < col_count - 1).astype(jnp.float32)[None, :, None], (plane_index > 0).astype(jnp.float32)[None, None, :], (plane_index < plane_count - 1).astype(jnp.float32)[None, None, :])

def face_terms(padded, face_masks, inverse_area):
    center = padded[:, 1:-1, 1:-1, 1:-1]
    neighbours = (padded[:, :-2, 1:-1, 1:-1], padded[:, 2:, 1:-1, 1:-1], padded[:, 1:-1, :-2, 1:-1], padded[:, 1:-1, 2:, 1:-1], padded[:, 1:-1, 1:-1, :-2], padded[:, 1:-1, 1:-1, 2:])
    weighted = jnp.zeros_like(center)
    weight_sum = jnp.zeros_like(center[0])
    for neighbour, face_mask in zip(neighbours, face_masks):
        change = neighbour - center
        spread = lax.optimization_barrier(jnp.sum(change * change, axis=0)) * inverse_area
        weight = face_mask / jnp.sqrt(1.0 + spread / (contrast * contrast))
        weighted = weighted + weight * neighbour
        weight_sum = weight_sum + weight
    return (center, weighted, weight_sum)

def solve_three(tensor, diagonal, right_side):
    main_aa = tensor[0] + diagonal
    cross_ab = tensor[1]
    cross_ac = tensor[2]
    main_bb = tensor[3] + diagonal
    cross_bc = tensor[4]
    main_cc = tensor[5] + diagonal
    cofactor_aa = main_bb * main_cc - cross_bc * cross_bc
    cofactor_ab = cross_ac * cross_bc - cross_ab * main_cc
    cofactor_ac = cross_ab * cross_bc - cross_ac * main_bb
    cofactor_bb = main_aa * main_cc - cross_ac * cross_ac
    cofactor_bc = cross_ab * cross_ac - main_aa * cross_bc
    cofactor_cc = main_aa * main_bb - cross_ab * cross_ab
    determinant = main_aa * cofactor_aa + cross_ab * cofactor_ab + cross_ac * cofactor_ac
    solved_a = (cofactor_aa * right_side[0] + cofactor_ab * right_side[1] + cofactor_ac * right_side[2]) / determinant
    solved_b = (cofactor_ab * right_side[0] + cofactor_bb * right_side[1] + cofactor_bc * right_side[2]) / determinant
    solved_c = (cofactor_ac * right_side[0] + cofactor_bc * right_side[1] + cofactor_cc * right_side[2]) / determinant
    return jnp.stack([solved_a, solved_b, solved_c])

def relax(padded, tensor, source, face_masks, inverse_area):
    center, weighted, weight_sum = face_terms(padded, face_masks, inverse_area)
    coupling = smoothness * inverse_area
    solved = solve_three(tensor, tikhonov + coupling * weight_sum, source + coupling * weighted)
    return center + relaxation * (solved - center)

def operate(padded, tensor, face_masks, inverse_area):
    center, weighted, weight_sum = face_terms(padded, face_masks, inverse_area)
    applied = jnp.stack([tensor[0] * center[0] + tensor[1] * center[1] + tensor[2] * center[2], tensor[1] * center[0] + tensor[3] * center[1] + tensor[4] * center[2], tensor[2] * center[0] + tensor[4] * center[1] + tensor[5] * center[2]])
    return applied + tikhonov * center + smoothness * inverse_area * (weight_sum * center - weighted)

def shrink(field):
    layers, height, across, planes = field.shape
    return field.reshape(layers, height // 2, 2, across // 2, 2, planes // 2, 2).mean(axis=(2, 4, 6))

def enlarge(field):
    layers, height, across, planes = field.shape
    spread_out = jnp.broadcast_to(field[:, :, None, :, None, :, None], (layers, height, 2, across, 2, planes, 2))
    return spread_out.reshape(layers, height * 2, across * 2, planes * 2)

def cycle(coarseness, flow_field, padded, source, tensors, mask_levels, extend):
    inverse_area = 0.25 ** coarseness
    tensor = tensors[coarseness]
    face_masks = mask_levels[coarseness]
    flow_field = relax(padded, tensor, source, face_masks, inverse_area)
    for repeat in range(SWEEPS - 1):
        flow_field = relax(extend(flow_field), tensor, source, face_masks, inverse_area)
    if coarseness == LEVELS - 1:
        return flow_field
    residue = source - operate(extend(flow_field), tensor, face_masks, inverse_area)
    coarse = shrink(flow_field)
    coarse_padded = extend(coarse)
    coarse_source = operate(coarse_padded, tensors[coarseness + 1], mask_levels[coarseness + 1], inverse_area * 0.25) + shrink(residue)
    solved = cycle(coarseness + 1, coarse, coarse_padded, coarse_source, tensors, mask_levels, extend)
    flow_field = flow_field + enlarge(solved - coarse)
    for repeat in range(SWEEPS):
        flow_field = relax(extend(flow_field), tensor, source, face_masks, inverse_area)
    return flow_field

def pad_flow(flow_field):
    return jnp.pad(flow_field, ((0, 0), (1, 1), (1, 1), (1, 1)))

def reference(first_frame, second_frame, source_column):
    brick_grid = second_frame.reshape(NY // BRICK, BRICK, NX // BRICK, BRICK, BCZ, BRICK).transpose(0, 2, 4, 1, 3, 5)
    column_table = source_column.reshape(N_GY, N_GX, BCY, BCX, BCZ).transpose(0, 2, 1, 3, 4).reshape(N_GY * BCY, N_GX * BCX, BCZ)
    row_ids = jnp.arange(N_GY * BCY, dtype=jnp.int32)[:, None, None]
    plane_ids = jnp.arange(BCZ, dtype=jnp.int32)[None, None, :]
    picked = brick_grid[row_ids, column_table, plane_ids]
    warped = picked.transpose(0, 3, 1, 4, 2, 5).reshape(NY, NX, NZ)
    average = 0.5 * (first_frame + warped)
    temporal = warped - first_frame
    tensor, source = motion_terms(jnp.pad(average, 1), temporal)
    tensors = [tensor]
    mask_levels = []
    for coarseness in range(LEVELS):
        if coarseness > 0:
            tensors.append(shrink(tensors[-1]))
        height = NY >> coarseness
        across = NX >> coarseness
        planes = NZ >> coarseness
        mask_levels.append(boundary_masks(jnp.arange(height, dtype=jnp.int32), height, jnp.arange(across, dtype=jnp.int32), across, jnp.arange(planes, dtype=jnp.int32), planes))
    flow_field = jnp.zeros((3, NY, NX, NZ), jnp.float32)
    padded = jnp.zeros((3, NY + 2, NX + 2, NZ + 2), jnp.float32)
    for repeat in range(CYCLES):
        if repeat > 0:
            padded = pad_flow(flow_field)
        flow_field = cycle(0, flow_field, padded, source, tensors, mask_levels, pad_flow)
    return flow_field
```

```python
import functools

import jax
import jax.numpy as jnp
from jax import lax
from jax.experimental import pallas as pl
from jax.experimental.pallas import tpu as pltpu
from jax.sharding import PartitionSpec as P

BRICK = 32
LEVELS = 4
TIKHONOV = 0.05
CONTRAST = 0.5
RELAXATION = 0.8
FLOOR = 1.0
LANES = 128
PAD = 8
ROWS = 4
LAYERS = 4
BUFFERS = (4, 6, 6, 3)
EXCHANGES = (4, 5, 5, 2)
MESH = pl.DeviceIdType.MESH


def dot(a, b):
    return jnp.dot(a, b, preferred_element_type=jnp.float32)


def two_terms(x, axis):
    high = x.astype(jnp.bfloat16).astype(jnp.float32)
    return jnp.concatenate([high, x - high], axis=axis).astype(jnp.bfloat16)


def solve_three(t, diagonal, f):
    aa = t[0] + diagonal
    ab, ac, bc = t[1], t[2], t[4]
    bb = t[3] + diagonal
    cc = t[5] + diagonal
    c_aa = bb * cc - bc * bc
    c_ab = ac * bc - ab * cc
    c_ac = ab * bc - ac * bb
    c_bb = aa * cc - ac * ac
    c_bc = ab * ac - aa * bc
    c_cc = aa * bb - ab * ab
    inverse = 1.0 / (aa * c_aa + ab * c_ab + ac * c_ac)
    return (
        (c_aa * f[0] + c_ab * f[1] + c_ac * f[2]) * inverse,
        (c_ab * f[0] + c_bb * f[1] + c_bc * f[2]) * inverse,
        (c_ac * f[0] + c_bc * f[1] + c_cc * f[2]) * inverse,
    )


def apply_three(t, u):
    return (
        t[0] * u[0] + t[1] * u[1] + t[2] * u[2],
        t[1] * u[0] + t[3] * u[1] + t[4] * u[2],
        t[2] * u[0] + t[4] * u[1] + t[5] * u[2],
    )


def kernel(n_gy, n_gx, height, across, *refs):
    first, second, columns, out = refs[:4]
    cols, packets_in, packets_out, avg, avg_stage, avg_halo = refs[4:10]
    refs = refs[2:]
    tensors = refs[8:12]
    sources = refs[12:16]
    iterates = refs[16:20]
    stages = refs[20:24]
    halos = refs[24:28]
    residues = refs[28:31]
    halo_send, halo_recv, avg_send, avg_recv, own_sem = refs[31:36]
    mine, table, picks, table_send, table_recv = refs[36:41]
    own_send, packet_send, col_recv, packet_recv, edge_send, edge_recv = refs[41:]
    my_y, my_x = lax.axis_index("gy"), lax.axis_index("gx")
    bases = [sum(EXCHANGES[:l]) * 4 for l in range(LEVELS)]
    hs = [height >> l for l in range(LEVELS)]
    ws = [across >> l for l in range(LEVELS)]
    wqs = [max(w, 8) for w in ws]

    for l in range(LEVELS):
        u, w, wq, h = iterates[l], ws[l], wqs[l], hs[l]
        for b in range(EXCHANGES[l]):
            zero_row = jnp.zeros((3, wq + 2 * PAD, LANES), jnp.float32)
            u[b, :, 0] = zero_row
            u[b, :, h + 1] = zero_row
            halos[l][b] = jnp.zeros(halos[l].shape[1:], jnp.float32)
    iterates[LEVELS - 1][...] = jnp.zeros(iterates[LEVELS - 1].shape, jnp.float32)
    avg[0] = jnp.zeros(avg.shape[1:], jnp.float32)
    avg[height + 1] = jnp.zeros(avg.shape[1:], jnp.float32)
    avg_halo[...] = jnp.zeros(avg_halo.shape, jnp.float32)

    has_up, has_down = my_y > 0, my_y < n_gy - 1
    has_left, has_right = my_x > 0, my_x < n_gx - 1
    up, down = (jnp.maximum(my_y - 1, 0), my_x), (jnp.minimum(my_y + 1, n_gy - 1), my_x)
    left, right = (my_y, jnp.maximum(my_x - 1, 0)), (my_y, jnp.minimum(my_x + 1, n_gx - 1))

    barrier = pltpu.get_barrier_semaphore()
    for step in range(1, n_gx):
        pl.semaphore_signal(
            barrier, inc=1, device_id=(my_y, lax.rem(my_x + step, n_gx)), device_id_type=MESH
        )
    for present, device in ((has_up, up), (has_down, down)):

        @pl.when(present)
        def _(device=device):
            pl.semaphore_signal(barrier, inc=1, device_id=device, device_id_type=MESH)

    peers = n_gx - 1 + jnp.where(has_up, 1, 0) + jnp.where(has_down, 1, 0)
    pl.semaphore_wait(barrier, peers)

    def to_peer(step, source, target, send, recv):
        return pltpu.make_async_remote_copy(
            src_ref=source,
            dst_ref=target,
            send_sem=send.at[step],
            recv_sem=recv.at[step],
            device_id=(my_y, lax.rem(my_x + step, n_gx)),
            device_id_type=MESH,
        )

    lane = lax.broadcasted_iota(jnp.int32, (8, LANES), 1)
    sub = lax.broadcasted_iota(jnp.int32, (8, LANES), 0)
    group = lax.broadcasted_iota(jnp.int32, (1, LANES), 1) // BRICK
    bricks = columns.shape[0]
    chunks = height // ROWS

    def ones(condition):
        return jnp.where(condition, 1.0, 0.0).astype(jnp.float32)

    def flag(condition):
        return jnp.where(condition, 1.0, 0.0).astype(jnp.float32)

    def remote(source, target, send, recv, device):
        return pltpu.make_async_remote_copy(
            src_ref=source,
            dst_ref=target,
            send_sem=send,
            recv_sem=recv,
            device_id=device,
            device_id_type=MESH,
        )

    def start_all(parts):
        for present, copy, _ in parts:

            @pl.when(present)
            def _(copy=copy):
                copy.start()

    def wait_all(parts):
        for present, copy, opposite in parts:

            @pl.when(present)
            def _(copy=copy, opposite=opposite):
                copy.wait_send()
                opposite.wait_recv()

    def rows_of(c):
        return pl.ds(c * ROWS, ROWS)

    def chunk_copy(source, target, send, recv, device):
        return remote(source, target, send, recv, device)

    layered = n_gx == 2 * LAYERS
    z, x = my_x // 2, my_x % 2
    inner = (z > 0) & (z < LAYERS - 1)
    ending = jnp.logical_not(inner)
    near = jnp.where(z == 0, 1, jnp.where(z == LAYERS - 1, LAYERS - 2, LAYERS - 1 - z))
    far = LAYERS - 1 - near
    end = jnp.where(z <= 1, 0, LAYERS - 1)

    def own_copies(c):
        rows = second.at[rows_of(c)]
        if not layered:
            return [
                (
                    None,
                    remote(
                        rows,
                        cols.at[my_x, rows_of(c)],
                        own_send.at[step, c],
                        col_recv.at[step, c],
                        (my_y, lax.rem(my_x + step, n_gx)),
                    ),
                )
                for step in range(1, n_gx)
            ]
        land = cols.at[z, rows_of(c)]
        return [
            (ending, remote(rows, land, own_send.at[1, c], col_recv.at[z, c], (my_y, 2 * far + x))),
            (None, remote(rows, land, own_send.at[0, c], col_recv.at[z, c], (my_y, 2 * near + x))),
            (ending, remote(rows, land, own_send.at[2, c], col_recv.at[z, c], (my_y, 2 * z + 1 - x))),
        ]

    def column_arrival(k, c):
        return remote(
            second.at[rows_of(c)],
            cols.at[k, rows_of(c)],
            own_send.at[0, c],
            col_recv.at[k, c],
            (my_y, lax.rem(my_x + 1, n_gx)),
        )

    def packet_copies(c):
        targets = [(my_y, 2 * end), (my_y, 2 * end + 1), (my_y, 2 * z + 1 - x)]
        return [
            remote(
                packets_out.at[i, rows_of(c)],
                packets_in.at[x, rows_of(c)],
                packet_send.at[i, c],
                packet_recv.at[x, c],
                device,
            )
            for i, device in enumerate(targets)
        ]

    def packet_arrival(k, c):
        return remote(
            packets_out.at[0, rows_of(c)],
            packets_in.at[k, rows_of(c)],
            packet_send.at[0, c],
            packet_recv.at[k, c],
            (my_y, lax.rem(my_x + 1, n_gx)),
        )

    def guarded(condition, act):
        if condition is None:
            act()
        else:
            pl.when(condition)(act)

    def send_own(t, carry):
        for condition, copy in own_copies((t + chunks - 1) % chunks):
            guarded(condition, copy.start)
        return carry

    for p in range(8):
        mine[pl.ds(p, 1)] = jnp.full((1, LANES), columns[min(p, bricks - 1)], jnp.int32)
    if layered:
        copies = [
            to_peer(step, mine, table.at[my_x], table_send, table_recv) for step in range(1, n_gx)
        ]
        for copy in copies:
            copy.start()
        keep = pltpu.make_async_copy(second, cols.at[z], own_sem)
        pl.when(inner)(keep.start)
    lax.fori_loop(0, chunks, send_own, 0)

    def wanted(entry):
        value = entry(0)
        for p in range(1, bricks):
            value = jnp.where(group == p, entry(p), value)
        return value

    picks[pl.ds(3, 1)] = wanted(lambda p: mine[pl.ds(p, 1)])
    if layered:
        pl.when(inner)(keep.wait)
        for copy in copies:
            copy.wait()
        for i, device in enumerate((2 * end, 2 * end + 1, 2 * z + 1 - x)):
            picks[pl.ds(i, 1)] = wanted(lambda p: table[device, pl.ds(p, 1)])

    def pick_of(i):
        return jnp.broadcast_to(picks[pl.ds(i, 1)], (across, LANES))

    def by_layer(values, layers):
        value = values[0]
        for k in range(1, LAYERS):
            value = jnp.where(layers == k, values[k], value)
        return value

    def forward(c):
        for k in range(LAYERS):

            @pl.when(z != k)
            def _(k=k):
                column_arrival(k, c).wait_recv()

        layers = [pick_of(i) // 2 for i in range(3)]
        for row in range(ROWS):
            r = c * ROWS + row
            values = [cols[k, r] for k in range(LAYERS)]
            for i in range(3):
                packets_out[i, r] = by_layer(values, layers[i])
        for copy in packet_copies(c):
            copy.start()

    def edges(c):
        return [
            (
                has_left,
                remote(avg_stage.at[c, 0], avg_halo.at[c, 1], edge_send.at[0, c], edge_recv.at[0, c], left),
                remote(avg_stage.at[c, 1], avg_halo.at[c, 0], edge_send.at[1, c], edge_recv.at[1, c], right),
            ),
            (
                has_right,
                remote(avg_stage.at[c, 1], avg_halo.at[c, 0], edge_send.at[1, c], edge_recv.at[1, c], right),
                remote(avg_stage.at[c, 0], avg_halo.at[c, 1], edge_send.at[0, c], edge_recv.at[0, c], left),
            ),
        ]

    def average(c, row, value):
        r = c * ROWS + row
        value = 0.5 * (first[r] + value)
        avg[r + 1, pl.ds(PAD, across)] = value
        avg_stage[c, 0, pl.ds(row, 1)] = value[0:1]
        avg_stage[c, 1, pl.ds(row, 1)] = value[across - 1 : across]

    def averages(c):
        pick = pick_of(3)
        if not layered:
            for step in range(1, n_gx):
                remote(
                    second.at[rows_of(c)],
                    cols.at[lax.rem(my_x - step + n_gx, n_gx), rows_of(c)],
                    own_send.at[step, c],
                    col_recv.at[step, c],
                    (my_y, lax.rem(my_x + step, n_gx)),
                ).wait_recv()
            for row in range(ROWS):
                value = second[c * ROWS + row]
                for step in range(1, n_gx):
                    k = lax.rem(my_x + step, n_gx)
                    value = jnp.where(pick == k, cols[k, c * ROWS + row], value)
                average(c, row, value)
        else:
            layer, side = pick // 2, pick % 2

            @pl.when(inner)
            def _():
                packet_arrival(1 - x, c).wait_recv()
                for row in range(ROWS):
                    r = c * ROWS + row
                    value = by_layer([cols[k, r] for k in range(LAYERS)], layer)
                    average(c, row, jnp.where(side == x, value, packets_in[1 - x, r]))

            @pl.when(ending)
            def _():
                column_arrival(z, c).wait_recv()
                for k in range(2):
                    packet_arrival(k, c).wait_recv()
                for row in range(ROWS):
                    r = c * ROWS + row
                    value = jnp.where(side == 0, packets_in[0, r], packets_in[1, r])
                    same = jnp.where(side == x, second[r], cols[z, r])
                    average(c, row, jnp.where(layer == z, same, value))

        for present, copy, _ in edges(c):
            pl.when(present)(copy.start)

    def place_average(c):
        for present, _, opposite in edges(c):
            pl.when(present)(opposite.wait_recv)
        for row in range(ROWS):
            r = c * ROWS + row
            avg[r + 1, pl.ds(PAD - 1, 1)] = avg_halo[c, 0, pl.ds(row, 1)]
            avg[r + 1, pl.ds(PAD + across, 1)] = avg_halo[c, 1, pl.ds(row, 1)]

    to_up = remote(avg.at[1], avg.at[height + 1], avg_send.at[0], avg_recv.at[0], up)
    to_down = remote(avg.at[height], avg.at[0], avg_send.at[1], avg_recv.at[1], down)
    row_parts = [(has_up, to_up, to_down), (has_down, to_down, to_up)]

    def row_flags(l, r):
        h = hs[l]
        at = my_y * h + r
        return flag(at > 0), flag(at < n_gy * h - 1)

    def masks_of(l):
        w, planes = ws[l], LANES >> l
        first_column = ones((sub > 0) | has_left)
        last_column = ones((sub != (w - 1) % 8) | has_right)
        below = ones((lane > 0) & (lane < planes))
        above = ones(lane < planes - 1)
        return first_column, last_column, below, above

    masks = [masks_of(l) for l in range(LEVELS)]

    def exchange(l, b):
        h, wq = hs[l], wqs[l]
        u, stage, halo = iterates[l], stages[l], halos[l]
        base = bases[l] + 4 * b
        inner = pl.ds(PAD, wq)
        send = [halo_send.at[base + d] for d in range(4)]
        recv = [halo_recv.at[base + d] for d in range(4)]
        to_up = remote(u.at[b, :, 1, inner], u.at[b, :, h + 1, inner], send[0], recv[0], up)
        to_down = remote(u.at[b, :, h, inner], u.at[b, :, 0, inner], send[1], recv[1], down)
        to_left = remote(stage.at[b, 0], halo.at[b, 1], send[2], recv[2], left)
        to_right = remote(stage.at[b, 1], halo.at[b, 0], send[3], recv[3], right)
        return [
            (has_up, to_up, to_down),
            (has_down, to_down, to_up),
            (has_left, to_left, to_right),
            (has_right, to_right, to_left),
        ]

    def place_halo(l, b, r):
        u, halo, w = iterates[l], halos[l], ws[l]
        for i in range(3):
            u[b, i, r + 1, pl.ds(PAD - 1, 1)] = halo[b, 0, i, pl.ds(r, 1)]
            u[b, i, r + 1, pl.ds(PAD + w, 1)] = halo[b, 1, i, pl.ds(r, 1)]

    def store_chunk(l, b, r, j, new):
        u, stage, w = iterates[l], stages[l], ws[l]
        for i in range(3):
            u[b, i, r + 1, pl.ds(PAD + 8 * j, 8)] = new[i]
            if b < EXCHANGES[l]:
                if j == 0:
                    stage[b, 0, i, pl.ds(r, 1)] = new[i][0:1]
                if j == wqs[l] // 8 - 1:
                    k = (w - 1) % 8
                    stage[b, 1, i, pl.ds(r, 1)] = new[i][k : k + 1]

    def faces(l, b, r, j, flags):
        u = iterates[l]
        s = PAD + 8 * j
        scale = 0.25**l / (CONTRAST * CONTRAST)
        first_column, last_column, below, above = masks[l]
        center = [u[b, i, r + 1, pl.ds(s, 8)] for i in range(3)]
        sides = [
            ([u[b, i, r, pl.ds(s, 8)] for i in range(3)], flags[0]),
            ([u[b, i, r + 2, pl.ds(s, 8)] for i in range(3)], flags[1]),
            (
                [u[b, i, r + 1, pl.ds(s - 1, 8)] for i in range(3)],
                first_column if j == 0 else None,
            ),
            (
                [u[b, i, r + 1, pl.ds(s + 1, 8)] for i in range(3)],
                last_column if j == wqs[l] // 8 - 1 else None,
            ),
            ([pltpu.roll(c, 1, 1) for c in center], below),
            ([pltpu.roll(c, LANES - 1, 1) for c in center], above),
        ]
        total, weighted = None, None
        for values, mask in sides:
            change = [v - c for v, c in zip(values, center)]
            spread = change[0] * change[0] + change[1] * change[1] + change[2] * change[2]
            weight = lax.rsqrt(1.0 + spread * scale)
            if mask is not None:
                weight = weight * mask
            terms = [weight * v for v in values]
            total = weight if total is None else total + weight
            weighted = terms if weighted is None else [a + t for a, t in zip(weighted, terms)]
        return center, weighted, total

    def row_loop(l, work):
        def step(r, carry):
            work(r)
            return carry

        lax.fori_loop(0, hs[l], step, 0)

    def grouped_loop(l, work):
        group = min(4, hs[l])

        def step(r, carry):
            for k in range(group):
                work(r * group + k)
            return carry

        lax.fori_loop(0, hs[l] // group, step, 0)

    def tensor_of(l, r, j):
        return [tensors[l][k, r, pl.ds(8 * j, 8)] for k in range(6)]

    def source_of(l, r, j):
        return [sources[l][k, r, pl.ds(8 * j, 8)] for k in range(3)]

    def relaxed(l, center, weighted, total, tensor, source):
        coupling = 0.25**l
        solved = solve_three(
            tensor,
            TIKHONOV + coupling * total,
            [f + coupling * q for f, q in zip(source, weighted)],
        )
        return [c + RELAXATION * (s - c) for c, s in zip(center, solved)]

    def applied(l, center, weighted, total, tensor):
        coupling = 0.25**l
        return [
            a + TIKHONOV * c + coupling * (total * c - q)
            for a, c, q in zip(apply_three(tensor, center), center, weighted)
        ]

    def chunk_loop(l, b, compute, store):
        chunks = wqs[l] // 8
        group = min(hs[l], max(1, 4 // chunks))

        def step(at, carry):
            rows = [at * group + k for k in range(group)]
            for r in rows:
                place_halo(l, b, r)
            results = []
            for r in rows:
                flags = row_flags(l, r)
                for j in range(chunks):
                    results.append((r, j, compute(r, j, flags)))
            for r, j, result in results:
                store(r, j, result)
            return carry

        lax.fori_loop(0, hs[l] // group, step, 0)

    def relax(l, b, target):
        def compute(r, j, flags):
            center, weighted, total = faces(l, b, r, j, flags)
            return relaxed(l, center, weighted, total, tensor_of(l, r, j), source_of(l, r, j))

        def store(r, j, new):
            if target is None:
                for i in range(3):
                    out[i, r, pl.ds(8 * j, 8)] = new[i]
            else:
                store_chunk(l, target, r, j, new)

        chunk_loop(l, b, compute, store)

    def residue(l, b):
        def compute(r, j, flags):
            center, weighted, total = faces(l, b, r, j, flags)
            value = applied(l, center, weighted, total, tensor_of(l, r, j))
            return [f - v for f, v in zip(source_of(l, r, j), value)]

        def store(r, j, new):
            for i in range(3):
                residues[l][i, r, pl.ds(8 * j, 8)] = new[i]

        chunk_loop(l, b, compute, store)

    def enter(l):
        def compute(r, j, flags):
            center, weighted, total = faces(l, 0, r, j, flags)
            tensor = tensor_of(l, r, j)
            value = applied(l, center, weighted, total, tensor)
            source = [f + v for f, v in zip(source_of(l, r, j), value)]
            return source, relaxed(l, center, weighted, total, tensor, source)

        def store(r, j, result):
            source, new = result
            for i in range(3):
                sources[l][i, r, pl.ds(8 * j, 8)] = source[i]
            store_chunk(l, 1, r, j, new)

        chunk_loop(l, 0, compute, store)

    def pair_matrix(rows, cols, fine_of, blocks):
        fine, coarse, coarse_padded = blocks
        i = lax.broadcasted_iota(jnp.int32, (rows, cols), 0)
        j = lax.broadcasted_iota(jnp.int32, (rows, cols), 1)
        f, c = (j, i) if fine_of == 1 else (i, j)
        return ones(
            (f // fine == c // coarse_padded)
            & ((f % fine) // 2 == c % coarse_padded)
            & (c % coarse_padded < coarse)
        )

    def doubled(matrix, axis):
        return jnp.concatenate([matrix, matrix], axis=axis).astype(jnp.bfloat16)

    lane_blocks = (LANES, LANES // 2, LANES)

    def shrink(l, count, fine_row, store):
        w, wc = wqs[l], wqs[l + 1]
        blocks = (w, ws[l + 1], wc)
        squeeze = doubled(pair_matrix(LANES, LANES, 0, lane_blocks), 0)
        join = doubled(pair_matrix(count * wc, count * w, 1, blocks), 1)

        def work(r):
            x = (fine_row(2 * r) + fine_row(2 * r + 1)).reshape(count * w, LANES)
            y = dot(join, two_terms(dot(two_terms(x, 1), squeeze), 0)) * 0.125
            store(r, y.reshape(count, wc, LANES))

        grouped_loop(l + 1, work)

    def shrink_iterate(l, b):
        u = iterates[l]
        coarse, stage, wc = iterates[l + 1], stages[l + 1], ws[l + 1]

        def store(r, y):
            coarse[0, :, r + 1, pl.ds(PAD, wqs[l + 1])] = y
            for i in range(3):
                stage[0, 0, i, pl.ds(r, 1)] = y[i, 0:1]
                stage[0, 1, i, pl.ds(r, 1)] = y[i, wc - 1 : wc]

        shrink(l, 3, lambda r: u[b, :, r + 1, pl.ds(PAD, wqs[l])], store)

    def shrink_array(l, count, fine, coarse):
        def store(r, y):
            coarse[:, r] = y

        shrink(l, count, lambda r: fine[:, r], store)

    def grow(l, b, solved, target):
        w, wc = wqs[l], wqs[l + 1]
        u, coarse, stage = iterates[l], iterates[l + 1], stages[l]
        spread = doubled(pair_matrix(LANES, LANES, 1, lane_blocks), 0)
        split = doubled(pair_matrix(3 * w, 3 * wc, 0, (w, ws[l + 1], wc)), 1)

        def work(r):
            inner = pl.ds(PAD, wc)
            if ws[l + 1] < wc:
                kept = lax.broadcasted_iota(jnp.int32, (3, wc, LANES), 1) < ws[l + 1]
                x = jnp.where(kept, coarse[solved, :, r + 1, inner] - coarse[0, :, r + 1, inner], 0.0)
            else:
                x = coarse[solved, :, r + 1, inner] - coarse[0, :, r + 1, inner]
            y = dot(two_terms(x.reshape(3 * wc, LANES), 1), spread)
            y = dot(split, two_terms(y, 0)).reshape(3, w, LANES)
            for row in range(2):
                at = 2 * r + row
                new = u[b, :, at + 1, pl.ds(PAD, w)] + y
                u[target, :, at + 1, pl.ds(PAD, w)] = new
                for i in range(3):
                    stage[target, 0, i, pl.ds(at, 1)] = new[i, 0:1]
                    stage[target, 1, i, pl.ds(at, 1)] = new[i, ws[l] - 1 : ws[l]]

        grouped_loop(l + 1, work)

    first_column, last_column, below, above = masks[0]

    def motion(r):
        flags = row_flags(0, r)
        for j in range(across // 8):
            s = PAD + 8 * j
            diffs, sums = [], []
            for shift in (-1, 0, 1):
                lower = avg[r, pl.ds(s + shift, 8)]
                middle = avg[r + 1, pl.ds(s + shift, 8)]
                upper = avg[r + 2, pl.ds(s + shift, 8)]
                diffs.append(0.5 * (upper - lower))
                sums.append(0.25 * (lower + 2.0 * middle + upper))
            along_rows = 0.25 * (diffs[0] + 2.0 * diffs[1] + diffs[2])
            along_cols = 0.5 * (sums[2] - sums[0])
            along_planes = 0.25 * (sums[0] + 2.0 * sums[1] + sums[2])

            def beside(x):
                return pltpu.roll(x, 1, 1) * below, pltpu.roll(x, LANES - 1, 1) * above

            def smooth(x):
                lower, upper = beside(x)
                return 0.25 * (lower + 2.0 * x + upper)

            g0, g1 = smooth(along_rows), smooth(along_cols)
            lower, upper = beside(along_planes)
            g2 = 0.5 * (upper - lower)
            normal = 1.0 / (g0 * g0 + g1 * g1 + g2 * g2 + FLOOR)
            n0, n1, n2 = g0 * normal, g1 * normal, g2 * normal
            tensor = [n0 * g0, n0 * g1, n0 * g2, n1 * g1, n1 * g2, n2 * g2]
            base = first[r, pl.ds(8 * j, 8)]
            temporal = 2.0 * (avg[r + 1, pl.ds(s, 8)] - base)
            source = [-n0 * temporal, -n1 * temporal, -n2 * temporal]
            for k in range(6):
                tensors[0][k, r, pl.ds(8 * j, 8)] = tensor[k]
            for k in range(3):
                sources[0][k, r, pl.ds(8 * j, 8)] = source[k]
            total = below + above + (flags[0] + flags[1])
            total = total + (first_column if j == 0 else 1.0)
            total = total + (last_column if j == across // 8 - 1 else 1.0)
            solved = solve_three(tensor, TIKHONOV + total, source)
            store_chunk(0, 0, r, j, [RELAXATION * x for x in solved])

    def motion_block(m):
        for row in range(ROWS):
            motion(m * ROWS + row)

    def gather_step(s, carry):
        def chunk_at(t):
            return (t + chunks - 1) % chunks

        if layered:
            pl.when(inner & (s < chunks))(lambda: forward(chunk_at(s)))
        pl.when((s >= 1) & (s <= chunks))(lambda: averages(chunk_at(s - 1)))
        pl.when(s >= 2)(lambda: place_average(chunk_at(s - 2)))
        pl.when(s == 3)(lambda: start_all(row_parts))
        pl.when(s >= 5)(lambda: motion_block(s - 4))

        @pl.when(s == chunks)
        def _():
            wait_all(row_parts)
            motion_block(0)
            for row in range(1, ROWS):
                motion(height - ROWS + row)

        return carry

    lax.fori_loop(0, chunks + 2, gather_step, 0)
    motion_block(chunks - 2)
    motion(height - ROWS)

    def finish_sends(c, carry):
        for condition, copy in own_copies(c):
            guarded(condition, copy.wait_send)
        if layered:
            for copy in packet_copies(c):
                pl.when(inner)(copy.wait_send)
        for present, copy, _ in edges(c):
            pl.when(present)(copy.wait_send)
        return carry

    lax.fori_loop(0, chunks, finish_sends, 0)

    current = exchange(0, 0)
    start_all(current)
    for l in range(LEVELS - 1):
        shrink_array(l, 6, tensors[l], tensors[l + 1])
    wait_all(current)
    relax(0, 0, 1)
    for l in range(LEVELS - 1):
        b = 1 if l == 0 else 2
        current = exchange(l, b)
        start_all(current)
        shrink_iterate(l, b)
        following = exchange(l + 1, 0)
        start_all(following)
        wait_all(current)
        residue(l, b)
        shrink_array(l, 3, residues[l], sources[l + 1])
        wait_all(following)
        enter(l + 1)
        current = exchange(l + 1, 1)
        start_all(current)
        wait_all(current)
        relax(l + 1, 1, 2)
    for l in range(LEVELS - 2, -1, -1):
        b = 1 if l == 0 else 2
        grow(l, b, 2 if l == LEVELS - 2 else 5, b + 1)
        for sweep in range(2):
            current = exchange(l, b + 1 + sweep)
            start_all(current)
            wait_all(current)
            last = l == 0 and sweep == 1
            relax(l, b + 1 + sweep, None if last else b + 2 + sweep)


def body(n_gy, n_gx, first_frame, second_frame, source_column):
    height, across, planes = first_frame.shape
    f32 = jnp.float32
    hs = [height >> l for l in range(LEVELS)]
    wqs = [max(across >> l, 8) for l in range(LEVELS)]
    hqs = [max(h, 8) for h in hs]
    total = sum(EXCHANGES) * 4
    vmem = pl.BlockSpec(memory_space=pltpu.VMEM)
    chunks = height // ROWS
    layered = n_gx == 2 * LAYERS
    volume = (height, across, LANES)
    scratch = [
        pltpu.VMEM((LAYERS if layered else n_gx, *volume), f32),
        pltpu.VMEM((2, *volume) if layered else (2, 8, LANES), f32),
        pltpu.VMEM((3, *volume) if layered else (3, 8, LANES), f32),
        pltpu.VMEM((height + 2, across + 2 * PAD, LANES), f32),
        pltpu.VMEM((chunks, 2, 8, LANES), f32),
        pltpu.VMEM((chunks, 2, 8, LANES), f32),
    ]
    scratch += [pltpu.VMEM((6, hs[l], wqs[l], LANES), f32) for l in range(LEVELS)]
    scratch += [pltpu.VMEM((3, hs[l], wqs[l], LANES), f32) for l in range(LEVELS)]
    scratch += [
        pltpu.VMEM((BUFFERS[l], 3, hs[l] + 2, wqs[l] + 2 * PAD, LANES), f32)
        for l in range(LEVELS)
    ]
    scratch += [pltpu.VMEM((EXCHANGES[l], 2, 3, hqs[l], LANES), f32) for l in range(LEVELS)] * 2
    scratch += [pltpu.VMEM((3, hs[l], wqs[l], LANES), f32) for l in range(LEVELS - 1)]
    dma = pltpu.SemaphoreType.DMA
    scratch += [dma((total,)), dma((total,)), dma((2,)), dma((2,)), dma]
    scratch += [
        pltpu.VMEM((8, LANES), jnp.int32),
        pltpu.VMEM((n_gx, 8, LANES), jnp.int32),
        pltpu.VMEM((8, LANES), jnp.int32),
        dma((n_gx,)),
        dma((n_gx,)),
        dma((3 if layered else n_gx, chunks)),
        dma((3, chunks)),
        dma((LAYERS if layered else n_gx, chunks)),
        dma((2, chunks)),
        dma((2, chunks)),
        dma((2, chunks)),
    ]
    columns = source_column.reshape(-1)
    return pl.pallas_call(
        functools.partial(kernel, n_gy, n_gx, height, across),
        out_shape=jax.ShapeDtypeStruct((3, height, across, planes), f32),
        in_specs=[vmem, vmem, pl.BlockSpec(memory_space=pltpu.SMEM)],
        out_specs=vmem,
        scratch_shapes=scratch,
        compiler_params=pltpu.CompilerParams(
            collective_id=0, has_side_effects=True, vmem_limit_bytes=56 * 1024 * 1024
        ),
    )(first_frame, second_frame, columns)


def solution(mesh):
    return jax.shard_map(
        functools.partial(body, mesh.shape["gy"], mesh.shape["gx"]),
        mesh=mesh,
        in_specs=(P("gy", "gx", None), P("gy", "gx", None), P("gy", "gx", None, None)),
        out_specs=P(None, "gy", "gx", None),
        check_vma=False,
    )
```

```python
import functools

import jax
import jax.numpy as jnp
from jax import lax
from jax.experimental import pallas as pl
from jax.experimental.pallas import tpu as pltpu
from jax.sharding import PartitionSpec as P

BRICK = 32
LEVELS = 4
TIKHONOV = 0.05
CONTRAST = 0.5
RELAXATION = 0.8
FLOOR = 1.0
LANES = 128
PAD = 8
ROWS = 4
LAYERS = 4
BUFFERS = (4, 6, 6, 3)
AHEAD = 2
MESH = pl.DeviceIdType.MESH


def dot(a, b):
    return jnp.dot(a, b, preferred_element_type=jnp.float32)


def two_terms(x, axis):
    high = x.astype(jnp.bfloat16).astype(jnp.float32)
    return jnp.concatenate([high, x - high], axis=axis).astype(jnp.bfloat16)


def solve_three(t, diagonal, f):
    aa = t[0] + diagonal
    ab, ac, bc = t[1], t[2], t[4]
    bb = t[3] + diagonal
    cc = t[5] + diagonal
    c_aa = bb * cc - bc * bc
    c_ab = ac * bc - ab * cc
    c_ac = ab * bc - ac * bb
    c_bb = aa * cc - ac * ac
    c_bc = ab * ac - aa * bc
    c_cc = aa * bb - ab * ab
    inverse = 1.0 / (aa * c_aa + ab * c_ab + ac * c_ac)
    return (
        (c_aa * f[0] + c_ab * f[1] + c_ac * f[2]) * inverse,
        (c_ab * f[0] + c_bb * f[1] + c_bc * f[2]) * inverse,
        (c_ac * f[0] + c_bc * f[1] + c_cc * f[2]) * inverse,
    )


def apply_three(t, u):
    return (
        t[0] * u[0] + t[1] * u[1] + t[2] * u[2],
        t[1] * u[0] + t[3] * u[1] + t[4] * u[2],
        t[2] * u[0] + t[4] * u[1] + t[5] * u[2],
    )


def kernel(n_gy, n_gx, height, across, *refs):
    first, second, columns, out = refs[:4]
    cols, packets_in, packets_out, avg, avg_stage, avg_halo = refs[4:10]
    refs = refs[2:]
    moved = refs[8]
    tensors = (None, *refs[9:12])
    sources = (None, *refs[12:15])
    refs = refs[:15] + (None,) + refs[15:]
    iterates = refs[16:20]
    stages = refs[20:24]
    halos = refs[24:28]
    residues = refs[28:31]
    halo_send, halo_recv, avg_send, avg_recv, own_sem = refs[31:36]
    mine, table, picks, table_send, table_recv = refs[36:41]
    own_send, packet_send, col_recv, packet_recv, edge_send, edge_recv = refs[41:]
    my_y, my_x = lax.axis_index("gy"), lax.axis_index("gx")
    bases = [sum(BUFFERS[:l]) * 4 for l in range(LEVELS)]
    hs = [height >> l for l in range(LEVELS)]
    ws = [across >> l for l in range(LEVELS)]
    wqs = [max(w, 8) for w in ws]

    for l in range(LEVELS):
        u, w, wq, h = iterates[l], ws[l], wqs[l], hs[l]
        for b in range(BUFFERS[l]):
            zero_row = jnp.zeros((3, wq + 2 * PAD, LANES), jnp.float32)
            u[b, :, 0] = zero_row
            u[b, :, h + 1] = zero_row
            halos[l][b] = jnp.zeros(halos[l].shape[1:], jnp.float32)
    iterates[LEVELS - 1][...] = jnp.zeros(iterates[LEVELS - 1].shape, jnp.float32)
    avg[0] = jnp.zeros(avg.shape[1:], jnp.float32)
    avg[height + 1] = jnp.zeros(avg.shape[1:], jnp.float32)
    avg_halo[...] = jnp.zeros(avg_halo.shape, jnp.float32)

    has_up, has_down = my_y > 0, my_y < n_gy - 1
    has_left, has_right = my_x > 0, my_x < n_gx - 1
    up, down = (jnp.maximum(my_y - 1, 0), my_x), (jnp.minimum(my_y + 1, n_gy - 1), my_x)
    left, right = (my_y, jnp.maximum(my_x - 1, 0)), (my_y, jnp.minimum(my_x + 1, n_gx - 1))

    barrier = pltpu.get_barrier_semaphore()
    for step in range(1, n_gx):
        pl.semaphore_signal(
            barrier, inc=1, device_id=(my_y, lax.rem(my_x + step, n_gx)), device_id_type=MESH
        )
    for present, device in ((has_up, up), (has_down, down)):

        @pl.when(present)
        def _(device=device):
            pl.semaphore_signal(barrier, inc=1, device_id=device, device_id_type=MESH)

    peers = n_gx - 1 + jnp.where(has_up, 1, 0) + jnp.where(has_down, 1, 0)
    pl.semaphore_wait(barrier, peers)

    def to_peer(step, source, target, send, recv):
        return pltpu.make_async_remote_copy(
            src_ref=source,
            dst_ref=target,
            send_sem=send.at[step],
            recv_sem=recv.at[step],
            device_id=(my_y, lax.rem(my_x + step, n_gx)),
            device_id_type=MESH,
        )

    lane = lax.broadcasted_iota(jnp.int32, (8, LANES), 1)
    sub = lax.broadcasted_iota(jnp.int32, (8, LANES), 0)
    group = lax.broadcasted_iota(jnp.int32, (1, LANES), 1) // BRICK
    bricks = columns.shape[0]
    chunks = height // ROWS

    def ones(condition):
        return jnp.where(condition, 1.0, 0.0).astype(jnp.float32)

    def flag(condition):
        return jnp.where(condition, 1.0, 0.0).astype(jnp.float32)

    def remote(source, target, send, recv, device):
        return pltpu.make_async_remote_copy(
            src_ref=source,
            dst_ref=target,
            send_sem=send,
            recv_sem=recv,
            device_id=device,
            device_id_type=MESH,
        )

    def start_all(parts):
        for present, copy, _ in parts:

            @pl.when(present)
            def _(copy=copy):
                copy.start()

    def wait_all(parts):
        for present, copy, opposite in parts:

            @pl.when(present)
            def _(copy=copy, opposite=opposite):
                copy.wait_send()
                opposite.wait_recv()

    def rows_of(c):
        return pl.ds(c * ROWS, ROWS)

    def chunk_copy(source, target, send, recv, device):
        return remote(source, target, send, recv, device)

    layered = n_gx == 2 * LAYERS
    z, x = my_x // 2, my_x % 2
    inner = (z > 0) & (z < LAYERS - 1)
    ending = jnp.logical_not(inner)
    near = jnp.where(z == 0, 1, jnp.where(z == LAYERS - 1, LAYERS - 2, LAYERS - 1 - z))
    far = LAYERS - 1 - near
    end = jnp.where(z <= 1, 0, LAYERS - 1)

    def own_copies(c):
        rows = second.at[rows_of(c)]
        if not layered:
            return [
                (
                    None,
                    remote(
                        rows,
                        cols.at[my_x, rows_of(c)],
                        own_send.at[step, c],
                        col_recv.at[step, c],
                        (my_y, lax.rem(my_x + step, n_gx)),
                    ),
                )
                for step in range(1, n_gx)
            ]
        land = cols.at[z, rows_of(c)]
        return [
            (ending, remote(rows, land, own_send.at[1, c], col_recv.at[z, c], (my_y, 2 * far + x))),
            (None, remote(rows, land, own_send.at[0, c], col_recv.at[z, c], (my_y, 2 * near + x))),
            (ending, remote(rows, land, own_send.at[2, c], col_recv.at[z, c], (my_y, 2 * z + 1 - x))),
        ]

    def column_arrival(k, c):
        return remote(
            second.at[rows_of(c)],
            cols.at[k, rows_of(c)],
            own_send.at[0, c],
            col_recv.at[k, c],
            (my_y, lax.rem(my_x + 1, n_gx)),
        )

    def packet_copies(c):
        targets = [(my_y, 2 * end), (my_y, 2 * end + 1), (my_y, 2 * z + 1 - x)]
        return [
            remote(
                packets_out.at[i, rows_of(c)],
                packets_in.at[x, rows_of(c)],
                packet_send.at[i, c],
                packet_recv.at[x, c],
                device,
            )
            for i, device in enumerate(targets)
        ]

    def packet_arrival(k, c):
        return remote(
            packets_out.at[0, rows_of(c)],
            packets_in.at[k, rows_of(c)],
            packet_send.at[0, c],
            packet_recv.at[k, c],
            (my_y, lax.rem(my_x + 1, n_gx)),
        )

    def guarded(condition, act):
        if condition is None:
            act()
        else:
            pl.when(condition)(act)

    def send_own(t, carry):
        for condition, copy in own_copies((t + chunks - 1) % chunks):
            guarded(condition, copy.start)
        return carry

    for p in range(8):
        mine[pl.ds(p, 1)] = jnp.full((1, LANES), columns[min(p, bricks - 1)], jnp.int32)
    if layered:
        copies = [
            to_peer(step, mine, table.at[my_x], table_send, table_recv) for step in range(1, n_gx)
        ]
        for copy in copies:
            copy.start()
        keep = pltpu.make_async_copy(second, cols.at[z], own_sem)
        pl.when(inner)(keep.start)
    lax.fori_loop(0, AHEAD, send_own, 0)

    def wanted(entry):
        value = entry(0)
        for p in range(1, bricks):
            value = jnp.where(group == p, entry(p), value)
        return value

    picks[pl.ds(3, 1)] = wanted(lambda p: mine[pl.ds(p, 1)])
    if layered:
        pl.when(inner)(keep.wait)
        for copy in copies:
            copy.wait()
        for i, device in enumerate((2 * end, 2 * end + 1, 2 * z + 1 - x)):
            picks[pl.ds(i, 1)] = wanted(lambda p: table[device, pl.ds(p, 1)])

    def pick_of(i):
        return jnp.broadcast_to(picks[pl.ds(i, 1)], (across, LANES))

    def by_layer(values, layers):
        value = values[0]
        for k in range(1, LAYERS):
            value = jnp.where(layers == k, values[k], value)
        return value

    def forward(c):
        for k in range(LAYERS):

            @pl.when(z != k)
            def _(k=k):
                column_arrival(k, c).wait_recv()

        layers = [pick_of(i) // 2 for i in range(3)]
        for row in range(ROWS):
            r = c * ROWS + row
            values = [cols[k, r] for k in range(LAYERS)]
            for i in range(3):
                packets_out[i, r] = by_layer(values, layers[i])
        for copy in packet_copies(c):
            copy.start()

    def edges(c):
        return [
            (
                has_left,
                remote(avg_stage.at[c, 0], avg_halo.at[c, 1], edge_send.at[0, c], edge_recv.at[0, c], left),
                remote(avg_stage.at[c, 1], avg_halo.at[c, 0], edge_send.at[1, c], edge_recv.at[1, c], right),
            ),
            (
                has_right,
                remote(avg_stage.at[c, 1], avg_halo.at[c, 0], edge_send.at[1, c], edge_recv.at[1, c], right),
                remote(avg_stage.at[c, 0], avg_halo.at[c, 1], edge_send.at[0, c], edge_recv.at[0, c], left),
            ),
        ]

    def average(c, row, value):
        r = c * ROWS + row
        value = 0.5 * (first[r] + value)
        avg[r + 1, pl.ds(PAD, across)] = value
        avg_stage[c, 0, pl.ds(row, 1)] = value[0:1]
        avg_stage[c, 1, pl.ds(row, 1)] = value[across - 1 : across]

    def averages(c):
        pick = pick_of(3)
        if not layered:
            for step in range(1, n_gx):
                remote(
                    second.at[rows_of(c)],
                    cols.at[lax.rem(my_x - step + n_gx, n_gx), rows_of(c)],
                    own_send.at[step, c],
                    col_recv.at[step, c],
                    (my_y, lax.rem(my_x + step, n_gx)),
                ).wait_recv()
            for row in range(ROWS):
                value = second[c * ROWS + row]
                for step in range(1, n_gx):
                    k = lax.rem(my_x + step, n_gx)
                    value = jnp.where(pick == k, cols[k, c * ROWS + row], value)
                average(c, row, value)
        else:
            layer, side = pick // 2, pick % 2

            @pl.when(inner)
            def _():
                packet_arrival(1 - x, c).wait_recv()
                for row in range(ROWS):
                    r = c * ROWS + row
                    value = by_layer([cols[k, r] for k in range(LAYERS)], layer)
                    average(c, row, jnp.where(side == x, value, packets_in[1 - x, r]))

            @pl.when(ending)
            def _():
                column_arrival(z, c).wait_recv()
                for k in range(2):
                    packet_arrival(k, c).wait_recv()
                for row in range(ROWS):
                    r = c * ROWS + row
                    value = jnp.where(side == 0, packets_in[0, r], packets_in[1, r])
                    same = jnp.where(side == x, second[r], cols[z, r])
                    average(c, row, jnp.where(layer == z, same, value))

        for present, copy, _ in edges(c):
            pl.when(present)(copy.start)

    def place_average(c):
        for present, _, opposite in edges(c):
            pl.when(present)(opposite.wait_recv)
        for row in range(ROWS):
            r = c * ROWS + row
            avg[r + 1, pl.ds(PAD - 1, 1)] = avg_halo[c, 0, pl.ds(row, 1)]
            avg[r + 1, pl.ds(PAD + across, 1)] = avg_halo[c, 1, pl.ds(row, 1)]

    to_up = remote(avg.at[1], avg.at[height + 1], avg_send.at[0], avg_recv.at[0], up)
    to_down = remote(avg.at[height], avg.at[0], avg_send.at[1], avg_recv.at[1], down)
    row_parts = [(has_up, to_up, to_down), (has_down, to_down, to_up)]

    def row_flags(l, r):
        h = hs[l]
        at = my_y * h + r
        return flag(at > 0), flag(at < n_gy * h - 1)

    def masks_of(l):
        w, planes = ws[l], LANES >> l
        first_column = ones((sub > 0) | has_left)
        last_column = ones((sub != (w - 1) % 8) | has_right)
        below = ones((lane > 0) & (lane < planes))
        above = ones(lane < planes - 1)
        return first_column, last_column, below, above

    masks = [masks_of(l) for l in range(LEVELS)]

    def exchange(l, b):
        h, wq = hs[l], wqs[l]
        u, stage, halo = iterates[l], stages[l], halos[l]
        base = bases[l] + 4 * b
        inner = pl.ds(PAD, wq)
        send = [halo_send.at[base + d] for d in range(4)]
        recv = [halo_recv.at[base + d] for d in range(4)]
        to_up = remote(u.at[b, :, 1, inner], u.at[b, :, h + 1, inner], send[0], recv[0], up)
        to_down = remote(u.at[b, :, h, inner], u.at[b, :, 0, inner], send[1], recv[1], down)
        to_left = remote(stage.at[b, 0], halo.at[b, 1], send[2], recv[2], left)
        to_right = remote(stage.at[b, 1], halo.at[b, 0], send[3], recv[3], right)
        return [
            (has_up, to_up, to_down),
            (has_down, to_down, to_up),
            (has_left, to_left, to_right),
            (has_right, to_right, to_left),
        ]

    def place_halo(l, b, r):
        u, halo, w = iterates[l], halos[l], ws[l]
        for i in range(3):
            u[b, i, r + 1, pl.ds(PAD - 1, 1)] = halo[b, 0, i, pl.ds(r, 1)]
            u[b, i, r + 1, pl.ds(PAD + w, 1)] = halo[b, 1, i, pl.ds(r, 1)]

    def store_chunk(l, b, r, j, new):
        u, stage, w = iterates[l], stages[l], ws[l]
        for i in range(3):
            u[b, i, r + 1, pl.ds(PAD + 8 * j, 8)] = new[i]
            if j == 0:
                stage[b, 0, i, pl.ds(r, 1)] = new[i][0:1]
            if j == wqs[l] // 8 - 1:
                k = (w - 1) % 8
                stage[b, 1, i, pl.ds(r, 1)] = new[i][k : k + 1]

    last_sub = sub == 7

    def sweep(l, b, start, count, js, group, compute, store):
        u = iterates[l]
        first_column, last_column, _, above = masks[l]
        end = wqs[l] // 8 - 1
        scale = 0.25**l / (CONTRAST * CONTRAST) / (4.0 if l == 0 else 1.0)

        def at(r, j, shift=0):
            return [u[b, i, r + 1, pl.ds(PAD + 8 * j + shift, 8)] for i in range(3)]

        def face(before, after, mask):
            change = [q - p for p, q in zip(before, after)]
            spread = change[0] * change[0] + change[1] * change[1] + change[2] * change[2]
            if scale != 1.0:
                spread = spread * scale
            weight = lax.rsqrt(1.0 + spread)
            if mask is not None:
                weight = weight * mask
            return [weight * c for c in change] + [weight]

        def row(r, carry):
            flags = row_flags(l, r)
            results, lower, previous = [], [], None
            for n, j in enumerate(js):
                center = at(r, j)
                down = face(center, at(r + 1, j), flags[1])
                lower.append(down)
                side = face(center, [pltpu.roll(c, LANES - 1, 1) for c in center], above)
                right = face(center, at(r, j, 1), last_column if j == end else None)
                if j - 1 in js:
                    left = [
                        pltpu.roll(jnp.where(last_sub, p, q), 1, 0) for p, q in zip(previous, right)
                    ]
                else:
                    left = face(at(r, j, -1), center, first_column if j == 0 else None)
                previous = right
                back = [pltpu.roll(v, 1, 1) for v in side]
                up = carry[n]
                flux = [
                    (down[i] - up[i]) + (side[i] - back[i]) + (right[i] - left[i]) for i in range(3)
                ]
                total = (down[3] + up[3]) + (side[3] + back[3]) + (right[3] + left[3])
                results.append(compute(r, j, center, flux, total))
            return results, lower

        def step(k, carry):
            base = start + k * group
            if 0 in js or end in js:
                for n in range(group):
                    place_halo(l, b, base + n)
            done = []
            for n in range(group):
                results, carry = row(base + n, carry)
                done.append(results)
            for n in range(group):
                for j, result in zip(js, done[n]):
                    store(base + n, j, result)
            return carry

        flags = row_flags(l, start)
        carry = [face(at(start - 1, j), at(start, j), flags[0]) for j in js]
        if count == group:
            step(0, carry)
        else:
            lax.fori_loop(0, count // group, step, carry)

    def part(l, b, which, compute, store):
        h = hs[l]
        every = tuple(range(wqs[l] // 8))
        if which == "all":
            sweep(l, b, 0, h, every, min(h, max(1, 4 // len(every))), compute, store)
        elif which == "edge":
            sweep(l, b, 0, h, (every[0], every[-1]), 2, compute, store)
            for r in (0, h - 1):
                sweep(l, b, r, 1, every[1:-1], 1, compute, store)
        else:
            sweep(l, b, 1, h - 2, every[1:-1], 2, compute, store)

    def motion_of(r, j):
        return [moved[k, r, pl.ds(8 * j, 8)] for k in range(5)]

    def tensor_of(l, r, j):
        return [tensors[l][k, r, pl.ds(8 * j, 8)] for k in range(6)]

    def source_of(l, r, j):
        return [sources[l][k, r, pl.ds(8 * j, 8)] for k in range(3)]

    def relax(l, b, target, which="all"):
        coupling = 0.25**l
        gain = 0.5 if target is None else 1.0

        def compute(r, j, center, flux, total):
            if l == 0:
                h0, h1, h2, time, hh = motion_of(r, j)
                around = [q + total * c for q, c in zip(flux, center)]
                diagonal = TIKHONOV + total
                widened = diagonal + hh
                common = h0 * around[0] + h1 * around[1] + h2 * around[2] + diagonal * time
                inverse = (gain * RELAXATION) / (diagonal * widened)
                keep = gain * (1.0 - RELAXATION)
                return [
                    keep * c + (q * widened - g * common) * inverse
                    for c, q, g in zip(center, around, (h0, h1, h2))
                ]
            solved = solve_three(
                tensor_of(l, r, j),
                TIKHONOV + coupling * total,
                [
                    f + coupling * (q + total * c)
                    for f, q, c in zip(source_of(l, r, j), flux, center)
                ],
            )
            return [c + RELAXATION * (s - c) for c, s in zip(center, solved)]

        def store(r, j, new):
            if target is None:
                for i in range(3):
                    out[i, r, pl.ds(8 * j, 8)] = new[i]
            else:
                store_chunk(l, target, r, j, new)

        part(l, b, which, compute, store)

    def residue(l, b, which="all"):
        coupling = 0.25**l

        def compute(r, j, center, flux, total):
            if l == 0:
                h0, h1, h2, time, _ = motion_of(r, j)
                common = h0 * center[0] + h1 * center[1] + h2 * center[2] + time
                return [
                    q - TIKHONOV * c - g * common for c, q, g in zip(center, flux, (h0, h1, h2))
                ]
            value = apply_three(tensor_of(l, r, j), center)
            return [
                f + coupling * q - TIKHONOV * c - a
                for f, q, c, a in zip(source_of(l, r, j), flux, center, value)
            ]

        def store(r, j, new):
            for i in range(3):
                residues[l][i, r, pl.ds(8 * j, 8)] = new[i]

        part(l, b, which, compute, store)

    def enter(l):
        coupling = 0.25**l

        def compute(r, j, center, flux, total):
            tensor, given = tensor_of(l, r, j), source_of(l, r, j)
            value = apply_three(tensor, center)
            source = [
                f + a + TIKHONOV * c - coupling * q
                for f, a, c, q in zip(given, value, center, flux)
            ]
            solved = solve_three(tensor, TIKHONOV + coupling * total, given)
            return source, [c + RELAXATION * s for c, s in zip(center, solved)]

        def store(r, j, result):
            source, new = result
            for i in range(3):
                sources[l][i, r, pl.ds(8 * j, 8)] = source[i]
            store_chunk(l, 1, r, j, new)

        part(l, 0, "all", compute, store)

    fine_lane = lax.broadcasted_iota(jnp.int32, (LANES, LANES), 0)
    coarse_lane = lax.broadcasted_iota(jnp.int32, (LANES, LANES), 1)
    halving = ones(fine_lane // 2 == coarse_lane)
    squeeze = jnp.concatenate([halving, halving], axis=0).astype(jnp.bfloat16)
    doubling = ones(coarse_lane // 2 == fine_lane)
    spread = jnp.concatenate([doubling, doubling], axis=0).astype(jnp.bfloat16)

    def corners(j, k, rest):
        return [
            (row, pl.ds(rest + 16 * j + parity, k, stride=2)) for row in range(2) for parity in range(2)
        ]

    def filled(x):
        if x.shape[0] == 8:
            return x
        return jnp.concatenate([x, jnp.zeros((8 - x.shape[0], LANES), jnp.float32)], axis=0)

    def shrink(l, rows, sums, factor, store):
        chunks = wqs[l + 1] // 8
        pieces = [[sums(r, j) for j in range(chunks)] for r in rows]
        flat = [filled(x) for of_row in pieces for of_chunk in of_row for x in of_chunk]
        y = dot(two_terms(jnp.concatenate(flat, axis=0), 1), squeeze) * factor
        at = 0
        for r in rows:
            for j in range(chunks):
                for i in range(len(pieces[0][0])):
                    store(r, j, i, y[8 * at : 8 * at + 8])
                    at += 1

    def summed(load, cells):
        values = [load(row, columns) for row, columns in cells]
        return (values[0] + values[1]) + (values[2] + values[3])

    def all_rows(l, work):
        group = min(4, hs[l])

        def step(k, carry):
            work([k * group + n for n in range(group)])
            return carry

        if hs[l] == group:
            step(0, 0)
        else:
            lax.fori_loop(0, hs[l] // group, step, 0)

    def shrink_iterate(l, b):
        u = iterates[l]
        coarse, stage, w = iterates[l + 1], stages[l + 1], ws[l + 1]
        k = min(8, w)

        def sums(r, j):
            cells = corners(j, k, PAD)
            return [
                summed(lambda row, columns, i=i: u[b, i, 2 * r + row + 1, columns], cells)
                for i in range(3)
            ]

        def store(r, j, i, y):
            coarse[0, i, r + 1, pl.ds(PAD + 8 * j, 8)] = y
            if j == 0:
                stage[0, 0, i, pl.ds(r, 1)] = y[0:1]
            if j == wqs[l + 1] // 8 - 1:
                n = (w - 1) % 8
                stage[0, 1, i, pl.ds(r, 1)] = y[n : n + 1]

        factor = 0.0625 if l == 0 else 0.125
        all_rows(l + 1, lambda rows: shrink(l, rows, sums, factor, store))

    def shrink_array(l, fine, coarse, factor):
        k = min(8, ws[l + 1])

        def sums(r, j):
            cells = corners(j, k, 0)
            return [
                summed(lambda row, columns, i=i: fine[i, 2 * r + row, columns], cells)
                for i in range(fine.shape[0])
            ]

        def store(r, j, i, y):
            coarse[i, r, pl.ds(8 * j, 8)] = y

        all_rows(l + 1, lambda rows: shrink(l, rows, sums, factor, store))

    def shrink_motion(rows):
        def sums(r, j):
            values = None
            for row, columns in corners(j, min(8, ws[1]), 0):
                h0, h1, h2 = [moved[k, 2 * r + row, columns] for k in range(3)]
                terms = [h0 * h0, h0 * h1, h0 * h2, h1 * h1, h1 * h2, h2 * h2]
                values = terms if values is None else [v + t for v, t in zip(values, terms)]
            return values

        def store(r, j, i, y):
            tensors[1][i, r, pl.ds(8 * j, 8)] = y

        shrink(0, rows, sums, 0.125, store)

    def grow(l, b, solved, target, arriving):
        wc, hc, h = wqs[l + 1], hs[l + 1], hs[l]
        kc, kr = min(8, ws[l + 1]), min(8, hc)
        u, coarse = iterates[l], iterates[l + 1]

        def spread_out(x):
            y = dot(two_terms(x, 1), spread)
            return 2.0 * y if l == 0 else y

        def correction(r):
            inner = pl.ds(PAD, wc)
            return (coarse[solved, :, r + 1, inner] - coarse[0, :, r + 1, inner]).reshape(3 * wc, LANES)

        def add(y, first_row, targets):
            for i in range(3):
                for j in range(wc // 8):
                    at = first_row + i * wc + 8 * j
                    piece = y[at : at + kc]
                    for row in targets:
                        for parity in range(2):
                            columns = pl.ds(PAD + 16 * j + parity, kc, stride=2)
                            u[target, i, row, columns] = u[b, i, row, columns] + piece

        def work(rows):
            y = spread_out(jnp.concatenate([correction(r) for r in rows], axis=0))
            for n, r in enumerate(rows):
                add(y, n * 3 * wc, (2 * r + 1, 2 * r + 2))

        all_rows(l + 1, work)
        wait_all(arriving)
        y = spread_out(jnp.concatenate([correction(-1), correction(hc)], axis=0))
        add(y, 0, (0,))
        add(y, 3 * wc, (h + 1,))
        hq = max(8, hc)
        halo, coarse_halo = halos[l], halos[l + 1]
        y = spread_out((coarse_halo[solved] - coarse_halo[0]).reshape(6 * hq, LANES))
        for side in range(2):
            for i in range(3):
                for j in range(hq // 8):
                    at = (side * 3 + i) * hq + 8 * j
                    for parity in range(2):
                        rows = pl.ds(16 * j + parity, kr, stride=2)
                        halo[target, side, i, rows] = halo[b, side, i, rows] + y[at : at + kr]

    first_column, last_column, below, above = masks[0]

    def motion(r):
        flags = row_flags(0, r)
        for j in range(across // 8):
            s = PAD + 8 * j
            diffs, sums = [], []
            for shift in (-1, 0, 1):
                lower = avg[r, pl.ds(s + shift, 8)]
                middle = avg[r + 1, pl.ds(s + shift, 8)]
                upper = avg[r + 2, pl.ds(s + shift, 8)]
                diffs.append(0.5 * (upper - lower))
                sums.append(0.25 * (lower + 2.0 * middle + upper))
            along_rows = 0.25 * (diffs[0] + 2.0 * diffs[1] + diffs[2])
            along_cols = 0.5 * (sums[2] - sums[0])
            along_planes = 0.25 * (sums[0] + 2.0 * sums[1] + sums[2])

            def beside(x):
                return pltpu.roll(x, 1, 1) * below, pltpu.roll(x, LANES - 1, 1) * above

            def smooth(x):
                lower, upper = beside(x)
                return 0.25 * (lower + 2.0 * x + upper)

            g0, g1 = smooth(along_rows), smooth(along_cols)
            lower, upper = beside(along_planes)
            g2 = 0.5 * (upper - lower)
            square = g0 * g0 + g1 * g1 + g2 * g2
            root = lax.rsqrt(square + FLOOR)
            h = [g0 * root, g1 * root, g2 * root]
            hh = square * root * root
            base = first[r, pl.ds(8 * j, 8)]
            time = (4.0 * root) * (avg[r + 1, pl.ds(s, 8)] - base)
            for k, value in enumerate((*h, time, hh)):
                moved[k, r, pl.ds(8 * j, 8)] = value
            total = below + above + (flags[0] + flags[1])
            total = total + (first_column if j == 0 else 1.0)
            total = total + (last_column if j == across // 8 - 1 else 1.0)
            length = time * (-RELAXATION / (TIKHONOV + total + hh))
            store_chunk(0, 0, r, j, [g * length for g in h])

    def shrink_block(m):
        shrink_motion([m * (ROWS // 2) + k for k in range(ROWS // 2)])

    def motion_block(m):
        for row in range(ROWS):
            motion(m * ROWS + row)
        shrink_block(m)

    def gather_step(s, carry):
        @pl.when(s + AHEAD < chunks)
        def _():
            send_own(s + AHEAD, 0)

        def chunk_at(t):
            return (t + chunks - 1) % chunks

        if layered:
            pl.when(inner & (s < chunks))(lambda: forward(chunk_at(s)))
        pl.when((s >= 1) & (s <= chunks))(lambda: averages(chunk_at(s - 1)))
        pl.when(s >= 2)(lambda: place_average(chunk_at(s - 2)))
        pl.when(s == 3)(lambda: start_all(row_parts))
        pl.when(s >= 5)(lambda: motion_block(s - 4))

        @pl.when(s == chunks)
        def _():
            wait_all(row_parts)
            motion_block(0)
            for row in range(1, ROWS):
                motion(height - ROWS + row)

        return carry

    lax.fori_loop(0, chunks + 2, gather_step, 0)
    for row in range(ROWS):
        motion((chunks - 2) * ROWS + row)
    motion(height - ROWS)
    arriving = exchange(0, 0)
    start_all(arriving)
    shrink_block(chunks - 2)
    shrink_block(chunks - 1)

    def finish_sends(c, carry):
        for condition, copy in own_copies(c):
            guarded(condition, copy.wait_send)
        if layered:
            for copy in packet_copies(c):
                pl.when(inner)(copy.wait_send)
        for present, copy, _ in edges(c):
            pl.when(present)(copy.wait_send)
        return carry

    lax.fori_loop(0, chunks, finish_sends, 0)
    for l in range(1, LEVELS - 1):
        shrink_array(l, tensors[l], tensors[l + 1], 0.125)
    relax(0, 0, 1, "inner")
    wait_all(arriving)
    relax(0, 0, 1, "edge")
    for l in range(LEVELS - 1):
        b = 1 if l == 0 else 2
        current = exchange(l, b)
        start_all(current)
        shrink_iterate(l, b)
        following = exchange(l + 1, 0)
        start_all(following)
        if l == 0:
            residue(l, b, "inner")
        wait_all(current)
        residue(l, b, "edge" if l == 0 else "all")
        shrink_array(l, residues[l], sources[l + 1], 0.0625 if l == 0 else 0.125)
        wait_all(following)
        enter(l + 1)
        current = exchange(l + 1, 1)
        start_all(current)
        wait_all(current)
        relax(l + 1, 1, 2)
    for l in range(LEVELS - 2, -1, -1):
        b = 1 if l == 0 else 2
        solved = 2 if l == LEVELS - 2 else 5
        arriving = exchange(l + 1, solved)
        start_all(arriving)
        grow(l, b, solved, b + 1, arriving)
        if l > 0:
            relax(l, b + 1, b + 2)
            current = exchange(l, b + 2)
            start_all(current)
            wait_all(current)
            relax(l, b + 2, b + 3)
    relax(0, 2, 3, "edge")
    current = exchange(0, 3)
    start_all(current)
    relax(0, 2, 3, "inner")
    relax(0, 3, None, "inner")
    wait_all(current)
    relax(0, 3, None, "edge")


def body(n_gy, n_gx, first_frame, second_frame, source_column):
    height, across, planes = first_frame.shape
    f32 = jnp.float32
    hs = [height >> l for l in range(LEVELS)]
    wqs = [max(across >> l, 8) for l in range(LEVELS)]
    hqs = [max(h, 8) for h in hs]
    total = sum(BUFFERS) * 4
    vmem = pl.BlockSpec(memory_space=pltpu.VMEM)
    chunks = height // ROWS
    layered = n_gx == 2 * LAYERS
    volume = (height, across, LANES)
    scratch = [
        pltpu.VMEM((LAYERS if layered else n_gx, *volume), f32),
        pltpu.VMEM((2, *volume) if layered else (2, 8, LANES), f32),
        pltpu.VMEM((3, *volume) if layered else (3, 8, LANES), f32),
        pltpu.VMEM((height + 2, across + 2 * PAD, LANES), f32),
        pltpu.VMEM((chunks, 2, 8, LANES), f32),
        pltpu.VMEM((chunks, 2, 8, LANES), f32),
    ]
    scratch += [pltpu.VMEM((6 if l else 5, hs[l], wqs[l], LANES), f32) for l in range(LEVELS)]
    scratch += [pltpu.VMEM((3, hs[l], wqs[l], LANES), f32) for l in range(1, LEVELS)]
    scratch += [
        pltpu.VMEM((BUFFERS[l], 3, hs[l] + 2, wqs[l] + 2 * PAD, LANES), f32)
        for l in range(LEVELS)
    ]
    scratch += [pltpu.VMEM((BUFFERS[l], 2, 3, hqs[l], LANES), f32) for l in range(LEVELS)] * 2
    scratch += [pltpu.VMEM((3, hs[l], wqs[l], LANES), f32) for l in range(LEVELS - 1)]
    dma = pltpu.SemaphoreType.DMA
    scratch += [dma((total,)), dma((total,)), dma((2,)), dma((2,)), dma]
    scratch += [
        pltpu.VMEM((8, LANES), jnp.int32),
        pltpu.VMEM((n_gx, 8, LANES), jnp.int32),
        pltpu.VMEM((8, LANES), jnp.int32),
        dma((n_gx,)),
        dma((n_gx,)),
        dma((3 if layered else n_gx, chunks)),
        dma((3, chunks)),
        dma((LAYERS if layered else n_gx, chunks)),
        dma((2, chunks)),
        dma((2, chunks)),
        dma((2, chunks)),
    ]
    columns = source_column.reshape(-1)
    return pl.pallas_call(
        functools.partial(kernel, n_gy, n_gx, height, across),
        out_shape=jax.ShapeDtypeStruct((3, height, across, planes), f32),
        in_specs=[vmem, vmem, pl.BlockSpec(memory_space=pltpu.SMEM)],
        out_specs=vmem,
        scratch_shapes=scratch,
        compiler_params=pltpu.CompilerParams(
            collective_id=0, has_side_effects=True, vmem_limit_bytes=56 * 1024 * 1024
        ),
    )(first_frame, second_frame, columns)


def solution(mesh):
    return jax.shard_map(
        functools.partial(body, mesh.shape["gy"], mesh.shape["gx"]),
        mesh=mesh,
        in_specs=(P("gy", "gx", None), P("gy", "gx", None), P("gy", "gx", None, None)),
        out_specs=P(None, "gy", "gx", None),
        check_vma=False,
    )
```

```python
import functools

import jax
import jax.numpy as jnp
from jax import lax
from jax.experimental import pallas as pl
from jax.experimental.pallas import tpu as pltpu
from jax.sharding import PartitionSpec as P

BRICK = 32
LEVELS = 4
TIKHONOV = 0.05
CONTRAST = 0.5
RELAXATION = 0.8
FLOOR = 1.0
LANES = 128
PAD = 8
ROWS = 4
LAYERS = 4
BUFFERS = (4, 6, 6, 3)
AHEAD = 2
CELLS = 16
MESH = pl.DeviceIdType.MESH


def dot(a, b):
    return jnp.dot(a, b, preferred_element_type=jnp.float32)


def two_terms(x, axis):
    high = x.astype(jnp.bfloat16).astype(jnp.float32)
    return jnp.concatenate([high, x - high], axis=axis).astype(jnp.bfloat16)


def solve_three(t, diagonal, f):
    aa = t[0] + diagonal
    ab, ac, bc = t[1], t[2], t[4]
    bb = t[3] + diagonal
    cc = t[5] + diagonal
    c_aa = bb * cc - bc * bc
    c_ab = ac * bc - ab * cc
    c_ac = ab * bc - ac * bb
    c_bb = aa * cc - ac * ac
    c_bc = ab * ac - aa * bc
    c_cc = aa * bb - ab * ab
    inverse = 1.0 / (aa * c_aa + ab * c_ab + ac * c_ac)
    return (
        (c_aa * f[0] + c_ab * f[1] + c_ac * f[2]) * inverse,
        (c_ab * f[0] + c_bb * f[1] + c_bc * f[2]) * inverse,
        (c_ac * f[0] + c_bc * f[1] + c_cc * f[2]) * inverse,
    )


def apply_three(t, u):
    return (
        t[0] * u[0] + t[1] * u[1] + t[2] * u[2],
        t[1] * u[0] + t[3] * u[1] + t[4] * u[2],
        t[2] * u[0] + t[4] * u[1] + t[5] * u[2],
    )


def kernel(n_gy, n_gx, height, across, *refs):
    first, second, columns, out = refs[:4]
    cols, packets_in, packets_out, avg, avg_stage, avg_halo = refs[4:10]
    refs = refs[2:]
    moved = refs[8]
    tensors = (None, *refs[9:12])
    sources = (None, *refs[12:15])
    refs = refs[:15] + (None,) + refs[15:]
    iterates = refs[16:20]
    stages = refs[20:24]
    halos = refs[24:28]
    residues = refs[28:31]
    halo_send, halo_recv, avg_send, avg_recv, own_sem = refs[31:36]
    mine, table, picks, table_send, table_recv = refs[36:41]
    own_send, packet_send, col_recv, packet_recv, edge_send, edge_recv = refs[41:]
    my_y, my_x = lax.axis_index("gy"), lax.axis_index("gx")
    bases = [sum(BUFFERS[:l]) * 4 for l in range(LEVELS)]
    hs = [height >> l for l in range(LEVELS)]
    ws = [across >> l for l in range(LEVELS)]
    wqs = [max(w, 8) for w in ws]

    for l in range(LEVELS):
        u, w, wq, h = iterates[l], ws[l], wqs[l], hs[l]
        for b in range(BUFFERS[l]):
            zero_row = jnp.zeros((3, wq + 2 * PAD, LANES), jnp.float32)
            u[b, :, 0] = zero_row
            u[b, :, h + 1] = zero_row
            halos[l][b] = jnp.zeros(halos[l].shape[1:], jnp.float32)
    iterates[LEVELS - 1][...] = jnp.zeros(iterates[LEVELS - 1].shape, jnp.float32)
    avg[0] = jnp.zeros(avg.shape[1:], jnp.float32)
    avg[height + 1] = jnp.zeros(avg.shape[1:], jnp.float32)
    avg_halo[...] = jnp.zeros(avg_halo.shape, jnp.float32)

    has_up, has_down = my_y > 0, my_y < n_gy - 1
    has_left, has_right = my_x > 0, my_x < n_gx - 1
    up, down = (jnp.maximum(my_y - 1, 0), my_x), (jnp.minimum(my_y + 1, n_gy - 1), my_x)
    left, right = (my_y, jnp.maximum(my_x - 1, 0)), (my_y, jnp.minimum(my_x + 1, n_gx - 1))

    barrier = pltpu.get_barrier_semaphore()
    for step in range(1, n_gx):
        pl.semaphore_signal(
            barrier, inc=1, device_id=(my_y, lax.rem(my_x + step, n_gx)), device_id_type=MESH
        )
    for present, device in ((has_up, up), (has_down, down)):

        @pl.when(present)
        def _(device=device):
            pl.semaphore_signal(barrier, inc=1, device_id=device, device_id_type=MESH)

    peers = n_gx - 1 + jnp.where(has_up, 1, 0) + jnp.where(has_down, 1, 0)
    pl.semaphore_wait(barrier, peers)

    def to_peer(step, source, target, send, recv):
        return pltpu.make_async_remote_copy(
            src_ref=source,
            dst_ref=target,
            send_sem=send.at[step],
            recv_sem=recv.at[step],
            device_id=(my_y, lax.rem(my_x + step, n_gx)),
            device_id_type=MESH,
        )

    lane = lax.broadcasted_iota(jnp.int32, (8, LANES), 1)
    sub = lax.broadcasted_iota(jnp.int32, (8, LANES), 0)
    group = lax.broadcasted_iota(jnp.int32, (1, LANES), 1) // BRICK
    bricks = columns.shape[0]
    chunks = height // ROWS

    def ones(condition):
        return jnp.where(condition, 1.0, 0.0).astype(jnp.float32)

    def flag(condition):
        return jnp.where(condition, 1.0, 0.0).astype(jnp.float32)

    def remote(source, target, send, recv, device):
        return pltpu.make_async_remote_copy(
            src_ref=source,
            dst_ref=target,
            send_sem=send,
            recv_sem=recv,
            device_id=device,
            device_id_type=MESH,
        )

    def start_all(parts):
        for present, copy, _ in parts:

            @pl.when(present)
            def _(copy=copy):
                copy.start()

    def wait_all(parts):
        for present, copy, opposite in parts:

            @pl.when(present)
            def _(copy=copy, opposite=opposite):
                copy.wait_send()
                opposite.wait_recv()

    def rows_of(c):
        return pl.ds(c * ROWS, ROWS)

    def chunk_copy(source, target, send, recv, device):
        return remote(source, target, send, recv, device)

    layered = n_gx == 2 * LAYERS
    z, x = my_x // 2, my_x % 2
    inner = (z > 0) & (z < LAYERS - 1)
    ending = jnp.logical_not(inner)
    near = jnp.where(z == 0, 1, jnp.where(z == LAYERS - 1, LAYERS - 2, LAYERS - 1 - z))
    far = LAYERS - 1 - near
    end = jnp.where(z <= 1, 0, LAYERS - 1)

    def own_copies(c):
        rows = second.at[rows_of(c)]
        if not layered:
            return [
                (
                    None,
                    remote(
                        rows,
                        cols.at[my_x, rows_of(c)],
                        own_send.at[step, c],
                        col_recv.at[step, c],
                        (my_y, lax.rem(my_x + step, n_gx)),
                    ),
                )
                for step in range(1, n_gx)
            ]
        land = cols.at[z, rows_of(c)]
        return [
            (ending, remote(rows, land, own_send.at[1, c], col_recv.at[z, c], (my_y, 2 * far + x))),
            (None, remote(rows, land, own_send.at[0, c], col_recv.at[z, c], (my_y, 2 * near + x))),
            (ending, remote(rows, land, own_send.at[2, c], col_recv.at[z, c], (my_y, 2 * z + 1 - x))),
        ]

    def column_arrival(k, c):
        return remote(
            second.at[rows_of(c)],
            cols.at[k, rows_of(c)],
            own_send.at[0, c],
            col_recv.at[k, c],
            (my_y, lax.rem(my_x + 1, n_gx)),
        )

    def packet_copies(c):
        targets = [(my_y, 2 * end), (my_y, 2 * end + 1), (my_y, 2 * z + 1 - x)]
        return [
            remote(
                packets_out.at[i, rows_of(c)],
                packets_in.at[x, rows_of(c)],
                packet_send.at[i, c],
                packet_recv.at[x, c],
                device,
            )
            for i, device in enumerate(targets)
        ]

    def packet_arrival(k, c):
        return remote(
            packets_out.at[0, rows_of(c)],
            packets_in.at[k, rows_of(c)],
            packet_send.at[0, c],
            packet_recv.at[k, c],
            (my_y, lax.rem(my_x + 1, n_gx)),
        )

    def guarded(condition, act):
        if condition is None:
            act()
        else:
            pl.when(condition)(act)

    def send_own(t, carry):
        for condition, copy in own_copies((t + chunks - 1) % chunks):
            guarded(condition, copy.start)
        return carry

    for p in range(8):
        mine[pl.ds(p, 1)] = jnp.full((1, LANES), columns[min(p, bricks - 1)], jnp.int32)
    if layered:
        copies = [
            to_peer(step, mine, table.at[my_x], table_send, table_recv) for step in range(1, n_gx)
        ]
        for copy in copies:
            copy.start()
        keep = pltpu.make_async_copy(second, cols.at[z], own_sem)
        pl.when(inner)(keep.start)
    lax.fori_loop(0, AHEAD, send_own, 0)

    def wanted(entry):
        value = entry(0)
        for p in range(1, bricks):
            value = jnp.where(group == p, entry(p), value)
        return value

    picks[pl.ds(3, 1)] = wanted(lambda p: mine[pl.ds(p, 1)])
    if layered:
        pl.when(inner)(keep.wait)
        for copy in copies:
            copy.wait()
        for i, device in enumerate((2 * end, 2 * end + 1, 2 * z + 1 - x)):
            picks[pl.ds(i, 1)] = wanted(lambda p: table[device, pl.ds(p, 1)])

    def pick_of(i):
        return jnp.broadcast_to(picks[pl.ds(i, 1)], (across, LANES))

    def by_layer(values, layers):
        value = values[0]
        for k in range(1, LAYERS):
            value = jnp.where(layers == k, values[k], value)
        return value

    def forward(c):
        for k in range(LAYERS):

            @pl.when(z != k)
            def _(k=k):
                column_arrival(k, c).wait_recv()

        layers = [pick_of(i) // 2 for i in range(3)]
        for row in range(ROWS):
            r = c * ROWS + row
            values = [cols[k, r] for k in range(LAYERS)]
            for i in range(3):
                packets_out[i, r] = by_layer(values, layers[i])
        for copy in packet_copies(c):
            copy.start()

    def edges(c):
        return [
            (
                has_left,
                remote(avg_stage.at[c, 0], avg_halo.at[c, 1], edge_send.at[0, c], edge_recv.at[0, c], left),
                remote(avg_stage.at[c, 1], avg_halo.at[c, 0], edge_send.at[1, c], edge_recv.at[1, c], right),
            ),
            (
                has_right,
                remote(avg_stage.at[c, 1], avg_halo.at[c, 0], edge_send.at[1, c], edge_recv.at[1, c], right),
                remote(avg_stage.at[c, 0], avg_halo.at[c, 1], edge_send.at[0, c], edge_recv.at[0, c], left),
            ),
        ]

    def average(c, row, value):
        r = c * ROWS + row
        value = 0.5 * (first[r] + value)
        avg[r + 1, pl.ds(PAD, across)] = value
        avg_stage[c, 0, pl.ds(row, 1)] = value[0:1]
        avg_stage[c, 1, pl.ds(row, 1)] = value[across - 1 : across]

    def averages(c):
        pick = pick_of(3)
        if not layered:
            for step in range(1, n_gx):
                remote(
                    second.at[rows_of(c)],
                    cols.at[lax.rem(my_x - step + n_gx, n_gx), rows_of(c)],
                    own_send.at[step, c],
                    col_recv.at[step, c],
                    (my_y, lax.rem(my_x + step, n_gx)),
                ).wait_recv()
            for row in range(ROWS):
                value = second[c * ROWS + row]
                for step in range(1, n_gx):
                    k = lax.rem(my_x + step, n_gx)
                    value = jnp.where(pick == k, cols[k, c * ROWS + row], value)
                average(c, row, value)
        else:
            layer, side = pick // 2, pick % 2

            @pl.when(inner)
            def _():
                packet_arrival(1 - x, c).wait_recv()
                for row in range(ROWS):
                    r = c * ROWS + row
                    value = by_layer([cols[k, r] for k in range(LAYERS)], layer)
                    average(c, row, jnp.where(side == x, value, packets_in[1 - x, r]))

            @pl.when(ending)
            def _():
                column_arrival(z, c).wait_recv()
                for k in range(2):
                    packet_arrival(k, c).wait_recv()
                for row in range(ROWS):
                    r = c * ROWS + row
                    value = jnp.where(side == 0, packets_in[0, r], packets_in[1, r])
                    same = jnp.where(side == x, second[r], cols[z, r])
                    average(c, row, jnp.where(layer == z, same, value))

        for present, copy, _ in edges(c):
            pl.when(present)(copy.start)

    def place_average(c):
        for present, _, opposite in edges(c):
            pl.when(present)(opposite.wait_recv)
        for row in range(ROWS):
            r = c * ROWS + row
            avg[r + 1, pl.ds(PAD - 1, 1)] = avg_halo[c, 0, pl.ds(row, 1)]
            avg[r + 1, pl.ds(PAD + across, 1)] = avg_halo[c, 1, pl.ds(row, 1)]

    to_up = remote(avg.at[1], avg.at[height + 1], avg_send.at[0], avg_recv.at[0], up)
    to_down = remote(avg.at[height], avg.at[0], avg_send.at[1], avg_recv.at[1], down)
    row_parts = [(has_up, to_up, to_down), (has_down, to_down, to_up)]

    def row_flags(l, r):
        h = hs[l]
        at = my_y * h + r
        return flag(at > 0), flag(at < n_gy * h - 1)

    def masks_of(l):
        w, planes = ws[l], LANES >> l
        first_column = ones((sub > 0) | has_left)
        last_column = ones((sub != (w - 1) % 8) | has_right)
        below = ones((lane > 0) & (lane < planes))
        above = ones(lane < planes - 1)
        return first_column, last_column, below, above

    masks = [masks_of(l) for l in range(LEVELS)]

    def exchange(l, b):
        h, wq = hs[l], wqs[l]
        u, stage, halo = iterates[l], stages[l], halos[l]
        base = bases[l] + 4 * b
        inner = pl.ds(PAD, wq)
        send = [halo_send.at[base + d] for d in range(4)]
        recv = [halo_recv.at[base + d] for d in range(4)]
        to_up = remote(u.at[b, :, 1, inner], u.at[b, :, h + 1, inner], send[0], recv[0], up)
        to_down = remote(u.at[b, :, h, inner], u.at[b, :, 0, inner], send[1], recv[1], down)
        to_left = remote(stage.at[b, 0], halo.at[b, 1], send[2], recv[2], left)
        to_right = remote(stage.at[b, 1], halo.at[b, 0], send[3], recv[3], right)
        return [
            (has_up, to_up, to_down),
            (has_down, to_down, to_up),
            (has_left, to_left, to_right),
            (has_right, to_right, to_left),
        ]

    def place_halo(l, b, r):
        u, halo, w = iterates[l], halos[l], ws[l]
        for i in range(3):
            u[b, i, r + 1, pl.ds(PAD - 1, 1)] = halo[b, 0, i, pl.ds(r, 1)]
            u[b, i, r + 1, pl.ds(PAD + w, 1)] = halo[b, 1, i, pl.ds(r, 1)]

    def store_chunk(l, b, r, j, new):
        u, stage, w = iterates[l], stages[l], ws[l]
        for i in range(3):
            u[b, i, r + 1, pl.ds(PAD + 8 * j, 8)] = new[i]
            if j == 0:
                stage[b, 0, i, pl.ds(r, 1)] = new[i][0:1]
            if j == wqs[l] // 8 - 1:
                k = (w - 1) % 8
                stage[b, 1, i, pl.ds(r, 1)] = new[i][k : k + 1]

    last_sub = sub == 7

    def sweep(l, b, start, count, js, group, compute, store):
        u = iterates[l]
        first_column, last_column, below, above = masks[l]
        end = wqs[l] // 8 - 1
        scale = 0.25**l / (CONTRAST * CONTRAST) / (4.0 if l == 0 else 1.0)

        def at(r, j, shift=0):
            return [u[b, i, r + 1, pl.ds(PAD + 8 * j + shift, 8)] for i in range(3)]

        def face(before, after, mask):
            change = [q - p for p, q in zip(before, after)]
            spread = change[0] * change[0] + change[1] * change[1] + change[2] * change[2]
            if scale != 1.0:
                spread = spread * scale
            weight = lax.rsqrt(1.0 + spread)
            if mask is not None:
                weight = weight * mask
            return [weight * c for c in change] + [weight]

        def row(r, carry):
            flags = row_flags(l, r)
            results, lower, previous = [], [], None
            for n, j in enumerate(js):
                center = at(r, j)
                down = face(center, at(r + 1, j), flags[1])
                lower.append(down)
                side = face(center, [pltpu.roll(c, LANES - 1, 1) for c in center], above)
                right = face(center, at(r, j, 1), last_column if j == end else None)
                if j - 1 in js:
                    left = [
                        pltpu.roll(jnp.where(last_sub, p, q), 1, 0) for p, q in zip(previous, right)
                    ]
                else:
                    left = face(at(r, j, -1), center, first_column if j == 0 else None)
                previous = right
                back = face([pltpu.roll(c, 1, 1) for c in center], center, below)
                up = carry[n]
                flux = [
                    (down[i] - up[i]) + (side[i] - back[i]) + (right[i] - left[i]) for i in range(3)
                ]
                total = (down[3] + up[3]) + (side[3] + back[3]) + (right[3] + left[3])
                results.append(compute(r, j, center, flux, total))
            return results, lower

        def step(k, carry):
            base = start + k * group
            if 0 in js or end in js:
                for n in range(group):
                    place_halo(l, b, base + n)
            done = []
            for n in range(group):
                results, carry = row(base + n, carry)
                done.append(results)
            for n in range(group):
                for j, result in zip(js, done[n]):
                    store(base + n, j, result)
            return carry

        flags = row_flags(l, start)
        carry = [face(at(start - 1, j), at(start, j), flags[0]) for j in js]
        if count == group:
            step(0, carry)
        else:
            lax.fori_loop(0, count // group, step, carry)

    def part(l, b, which, compute, store):
        h = hs[l]
        every = tuple(range(wqs[l] // 8))
        if which == "all":
            sweep(l, b, 0, h, every, min(h, max(1, CELLS // len(every))), compute, store)
        elif which == "edge":
            sweep(l, b, 0, h, (every[0], every[-1]), CELLS // 2, compute, store)
            for r in (0, h - 1):
                sweep(l, b, r, 1, every[1:-1], 1, compute, store)
        else:
            sweep(l, b, 1, h - 2, every[1:-1], 6, compute, store)

    def motion_of(r, j):
        return [moved[k, r, pl.ds(8 * j, 8)] for k in range(5)]

    def tensor_of(l, r, j):
        return [tensors[l][k, r, pl.ds(8 * j, 8)] for k in range(6)]

    def source_of(l, r, j):
        return [sources[l][k, r, pl.ds(8 * j, 8)] for k in range(3)]

    def relax(l, b, target, which="all"):
        coupling = 0.25**l
        gain = 0.5 if target is None else 1.0

        def compute(r, j, center, flux, total):
            if l == 0:
                h0, h1, h2, time, hh = motion_of(r, j)
                around = [q + total * c for q, c in zip(flux, center)]
                diagonal = TIKHONOV + total
                widened = diagonal + hh
                common = h0 * around[0] + h1 * around[1] + h2 * around[2] + diagonal * time
                inverse = (gain * RELAXATION) / (diagonal * widened)
                keep = gain * (1.0 - RELAXATION)
                return [
                    keep * c + (q * widened - g * common) * inverse
                    for c, q, g in zip(center, around, (h0, h1, h2))
                ]
            solved = solve_three(
                tensor_of(l, r, j),
                TIKHONOV + coupling * total,
                [
                    f + coupling * (q + total * c)
                    for f, q, c in zip(source_of(l, r, j), flux, center)
                ],
            )
            return [c + RELAXATION * (s - c) for c, s in zip(center, solved)]

        def store(r, j, new):
            if target is None:
                for i in range(3):
                    out[i, r, pl.ds(8 * j, 8)] = new[i]
            else:
                store_chunk(l, target, r, j, new)

        part(l, b, which, compute, store)

    def residue(l, b, which="all"):
        coupling = 0.25**l

        def compute(r, j, center, flux, total):
            if l == 0:
                h0, h1, h2, time, _ = motion_of(r, j)
                common = h0 * center[0] + h1 * center[1] + h2 * center[2] + time
                return [
                    q - TIKHONOV * c - g * common for c, q, g in zip(center, flux, (h0, h1, h2))
                ]
            value = apply_three(tensor_of(l, r, j), center)
            return [
                f + coupling * q - TIKHONOV * c - a
                for f, q, c, a in zip(source_of(l, r, j), flux, center, value)
            ]

        def store(r, j, new):
            for i in range(3):
                residues[l][i, r, pl.ds(8 * j, 8)] = new[i]

        part(l, b, which, compute, store)

    def enter(l):
        coupling = 0.25**l

        def compute(r, j, center, flux, total):
            tensor, given = tensor_of(l, r, j), source_of(l, r, j)
            value = apply_three(tensor, center)
            source = [
                f + a + TIKHONOV * c - coupling * q
                for f, a, c, q in zip(given, value, center, flux)
            ]
            solved = solve_three(tensor, TIKHONOV + coupling * total, given)
            return source, [c + RELAXATION * s for c, s in zip(center, solved)]

        def store(r, j, result):
            source, new = result
            for i in range(3):
                sources[l][i, r, pl.ds(8 * j, 8)] = source[i]
            store_chunk(l, 1, r, j, new)

        part(l, 0, "all", compute, store)

    fine_lane = lax.broadcasted_iota(jnp.int32, (LANES, LANES), 0)
    coarse_lane = lax.broadcasted_iota(jnp.int32, (LANES, LANES), 1)
    halving = ones(fine_lane // 2 == coarse_lane)
    squeeze = jnp.concatenate([halving, halving], axis=0).astype(jnp.bfloat16)
    doubling = ones(coarse_lane // 2 == fine_lane)
    spread = jnp.concatenate([doubling, doubling], axis=0).astype(jnp.bfloat16)

    def corners(j, k, rest):
        return [
            (row, pl.ds(rest + 16 * j + parity, k, stride=2)) for row in range(2) for parity in range(2)
        ]

    def filled(x):
        if x.shape[0] == 8:
            return x
        return jnp.concatenate([x, jnp.zeros((8 - x.shape[0], LANES), jnp.float32)], axis=0)

    def shrink(l, rows, sums, factor, store):
        chunks = wqs[l + 1] // 8
        pieces = [[sums(r, j) for j in range(chunks)] for r in rows]
        flat = [filled(x) for of_row in pieces for of_chunk in of_row for x in of_chunk]
        y = dot(two_terms(jnp.concatenate(flat, axis=0), 1), squeeze) * factor
        at = 0
        for r in rows:
            for j in range(chunks):
                for i in range(len(pieces[0][0])):
                    store(r, j, i, y[8 * at : 8 * at + 8])
                    at += 1

    def summed(load, cells):
        values = [load(row, columns) for row, columns in cells]
        return (values[0] + values[1]) + (values[2] + values[3])

    def all_rows(l, work):
        group = min(4, hs[l])

        def step(k, carry):
            work([k * group + n for n in range(group)])
            return carry

        if hs[l] == group:
            step(0, 0)
        else:
            lax.fori_loop(0, hs[l] // group, step, 0)

    def shrink_iterate(l, b):
        u = iterates[l]
        coarse, stage, w = iterates[l + 1], stages[l + 1], ws[l + 1]
        k = min(8, w)

        def sums(r, j):
            cells = corners(j, k, PAD)
            return [
                summed(lambda row, columns, i=i: u[b, i, 2 * r + row + 1, columns], cells)
                for i in range(3)
            ]

        def store(r, j, i, y):
            coarse[0, i, r + 1, pl.ds(PAD + 8 * j, 8)] = y
            if j == 0:
                stage[0, 0, i, pl.ds(r, 1)] = y[0:1]
            if j == wqs[l + 1] // 8 - 1:
                n = (w - 1) % 8
                stage[0, 1, i, pl.ds(r, 1)] = y[n : n + 1]

        factor = 0.0625 if l == 0 else 0.125
        all_rows(l + 1, lambda rows: shrink(l, rows, sums, factor, store))

    def shrink_array(l, fine, coarse, factor):
        k = min(8, ws[l + 1])

        def sums(r, j):
            cells = corners(j, k, 0)
            return [
                summed(lambda row, columns, i=i: fine[i, 2 * r + row, columns], cells)
                for i in range(fine.shape[0])
            ]

        def store(r, j, i, y):
            coarse[i, r, pl.ds(8 * j, 8)] = y

        all_rows(l + 1, lambda rows: shrink(l, rows, sums, factor, store))

    def shrink_motion(rows):
        def sums(r, j):
            values = None
            for row, columns in corners(j, min(8, ws[1]), 0):
                h0, h1, h2 = [moved[k, 2 * r + row, columns] for k in range(3)]
                terms = [h0 * h0, h0 * h1, h0 * h2, h1 * h1, h1 * h2, h2 * h2]
                values = terms if values is None else [v + t for v, t in zip(values, terms)]
            return values

        def store(r, j, i, y):
            tensors[1][i, r, pl.ds(8 * j, 8)] = y

        shrink(0, rows, sums, 0.125, store)

    def grow(l, b, solved, target, arriving):
        wc, hc, h = wqs[l + 1], hs[l + 1], hs[l]
        kc, kr = min(8, ws[l + 1]), min(8, hc)
        u, coarse = iterates[l], iterates[l + 1]

        def spread_out(x):
            y = dot(two_terms(x, 1), spread)
            return 2.0 * y if l == 0 else y

        def correction(r):
            inner = pl.ds(PAD, wc)
            return (coarse[solved, :, r + 1, inner] - coarse[0, :, r + 1, inner]).reshape(3 * wc, LANES)

        def add(y, first_row, targets):
            for i in range(3):
                for j in range(wc // 8):
                    at = first_row + i * wc + 8 * j
                    piece = y[at : at + kc]
                    for row in targets:
                        for parity in range(2):
                            columns = pl.ds(PAD + 16 * j + parity, kc, stride=2)
                            u[target, i, row, columns] = u[b, i, row, columns] + piece

        def work(rows):
            y = spread_out(jnp.concatenate([correction(r) for r in rows], axis=0))
            for n, r in enumerate(rows):
                add(y, n * 3 * wc, (2 * r + 1, 2 * r + 2))

        all_rows(l + 1, work)
        wait_all(arriving)
        y = spread_out(jnp.concatenate([correction(-1), correction(hc)], axis=0))
        add(y, 0, (0,))
        add(y, 3 * wc, (h + 1,))
        hq = max(8, hc)
        halo, coarse_halo = halos[l], halos[l + 1]
        y = spread_out((coarse_halo[solved] - coarse_halo[0]).reshape(6 * hq, LANES))
        for side in range(2):
            for i in range(3):
                for j in range(hq // 8):
                    at = (side * 3 + i) * hq + 8 * j
                    for parity in range(2):
                        rows = pl.ds(16 * j + parity, kr, stride=2)
                        halo[target, side, i, rows] = halo[b, side, i, rows] + y[at : at + kr]

    first_column, last_column, below, above = masks[0]

    def motion(r):
        flags = row_flags(0, r)
        for j in range(across // 8):
            s = PAD + 8 * j
            diffs, sums = [], []
            for shift in (-1, 0, 1):
                lower = avg[r, pl.ds(s + shift, 8)]
                middle = avg[r + 1, pl.ds(s + shift, 8)]
                upper = avg[r + 2, pl.ds(s + shift, 8)]
                diffs.append(0.5 * (upper - lower))
                sums.append(0.25 * (lower + 2.0 * middle + upper))
            along_rows = 0.25 * (diffs[0] + 2.0 * diffs[1] + diffs[2])
            along_cols = 0.5 * (sums[2] - sums[0])
            along_planes = 0.25 * (sums[0] + 2.0 * sums[1] + sums[2])

            def beside(x):
                return pltpu.roll(x, 1, 1) * below, pltpu.roll(x, LANES - 1, 1) * above

            def smooth(x):
                lower, upper = beside(x)
                return 0.25 * (lower + 2.0 * x + upper)

            g0, g1 = smooth(along_rows), smooth(along_cols)
            lower, upper = beside(along_planes)
            g2 = 0.5 * (upper - lower)
            square = g0 * g0 + g1 * g1 + g2 * g2
            root = lax.rsqrt(square + FLOOR)
            h = [g0 * root, g1 * root, g2 * root]
            hh = square * root * root
            base = first[r, pl.ds(8 * j, 8)]
            time = (4.0 * root) * (avg[r + 1, pl.ds(s, 8)] - base)
            for k, value in enumerate((*h, time, hh)):
                moved[k, r, pl.ds(8 * j, 8)] = value
            total = below + above + (flags[0] + flags[1])
            total = total + (first_column if j == 0 else 1.0)
            total = total + (last_column if j == across // 8 - 1 else 1.0)
            length = time * (-RELAXATION / (TIKHONOV + total + hh))
            store_chunk(0, 0, r, j, [g * length for g in h])

    def shrink_block(m):
        shrink_motion([m * (ROWS // 2) + k for k in range(ROWS // 2)])

    def motion_block(m):
        for row in range(ROWS):
            motion(m * ROWS + row)
        shrink_block(m)

    def gather_step(s, carry):
        @pl.when(s + AHEAD < chunks)
        def _():
            send_own(s + AHEAD, 0)

        def chunk_at(t):
            return (t + chunks - 1) % chunks

        if layered:
            pl.when(inner & (s < chunks))(lambda: forward(chunk_at(s)))
        pl.when((s >= 1) & (s <= chunks))(lambda: averages(chunk_at(s - 1)))
        pl.when(s >= 2)(lambda: place_average(chunk_at(s - 2)))
        pl.when(s == 3)(lambda: start_all(row_parts))
        pl.when(s >= 5)(lambda: motion_block(s - 4))

        @pl.when(s == chunks)
        def _():
            wait_all(row_parts)
            motion_block(0)
            for row in range(1, ROWS):
                motion(height - ROWS + row)

        return carry

    lax.fori_loop(0, chunks + 2, gather_step, 0)
    for row in range(ROWS):
        motion((chunks - 2) * ROWS + row)
    motion(height - ROWS)
    arriving = exchange(0, 0)
    start_all(arriving)
    shrink_block(chunks - 2)
    shrink_block(chunks - 1)

    def finish_sends(c, carry):
        for condition, copy in own_copies(c):
            guarded(condition, copy.wait_send)
        if layered:
            for copy in packet_copies(c):
                pl.when(inner)(copy.wait_send)
        for present, copy, _ in edges(c):
            pl.when(present)(copy.wait_send)
        return carry

    lax.fori_loop(0, chunks, finish_sends, 0)
    for l in range(1, LEVELS - 1):
        shrink_array(l, tensors[l], tensors[l + 1], 0.125)
    relax(0, 0, 1, "inner")
    wait_all(arriving)
    relax(0, 0, 1, "edge")
    for l in range(LEVELS - 1):
        b = 1 if l == 0 else 2
        current = exchange(l, b)
        start_all(current)
        shrink_iterate(l, b)
        following = exchange(l + 1, 0)
        start_all(following)
        if l == 0:
            residue(l, b, "inner")
        wait_all(current)
        residue(l, b, "edge" if l == 0 else "all")
        shrink_array(l, residues[l], sources[l + 1], 0.0625 if l == 0 else 0.125)
        wait_all(following)
        enter(l + 1)
        current = exchange(l + 1, 1)
        start_all(current)
        wait_all(current)
        relax(l + 1, 1, 2)
    for l in range(LEVELS - 2, -1, -1):
        b = 1 if l == 0 else 2
        solved = 2 if l == LEVELS - 2 else 5
        arriving = exchange(l + 1, solved)
        start_all(arriving)
        grow(l, b, solved, b + 1, arriving)
        if l > 0:
            relax(l, b + 1, b + 2)
            current = exchange(l, b + 2)
            start_all(current)
            wait_all(current)
            relax(l, b + 2, b + 3)
    relax(0, 2, 3, "edge")
    current = exchange(0, 3)
    start_all(current)
    relax(0, 2, 3, "inner")
    relax(0, 3, None, "inner")
    wait_all(current)
    relax(0, 3, None, "edge")


def body(n_gy, n_gx, first_frame, second_frame, source_column):
    height, across, planes = first_frame.shape
    f32 = jnp.float32
    hs = [height >> l for l in range(LEVELS)]
    wqs = [max(across >> l, 8) for l in range(LEVELS)]
    hqs = [max(h, 8) for h in hs]
    total = sum(BUFFERS) * 4
    vmem = pl.BlockSpec(memory_space=pltpu.VMEM)
    chunks = height // ROWS
    layered = n_gx == 2 * LAYERS
    volume = (height, across, LANES)
    scratch = [
        pltpu.VMEM((LAYERS if layered else n_gx, *volume), f32),
        pltpu.VMEM((2, *volume) if layered else (2, 8, LANES), f32),
        pltpu.VMEM((3, *volume) if layered else (3, 8, LANES), f32),
        pltpu.VMEM((height + 2, across + 2 * PAD, LANES), f32),
        pltpu.VMEM((chunks, 2, 8, LANES), f32),
        pltpu.VMEM((chunks, 2, 8, LANES), f32),
    ]
    scratch += [pltpu.VMEM((6 if l else 5, hs[l], wqs[l], LANES), f32) for l in range(LEVELS)]
    scratch += [pltpu.VMEM((3, hs[l], wqs[l], LANES), f32) for l in range(1, LEVELS)]
    scratch += [
        pltpu.VMEM((BUFFERS[l], 3, hs[l] + 2, wqs[l] + 2 * PAD, LANES), f32)
        for l in range(LEVELS)
    ]
    scratch += [pltpu.VMEM((BUFFERS[l], 2, 3, hqs[l], LANES), f32) for l in range(LEVELS)] * 2
    scratch += [pltpu.VMEM((3, hs[l], wqs[l], LANES), f32) for l in range(LEVELS - 1)]
    dma = pltpu.SemaphoreType.DMA
    scratch += [dma((total,)), dma((total,)), dma((2,)), dma((2,)), dma]
    scratch += [
        pltpu.VMEM((8, LANES), jnp.int32),
        pltpu.VMEM((n_gx, 8, LANES), jnp.int32),
        pltpu.VMEM((8, LANES), jnp.int32),
        dma((n_gx,)),
        dma((n_gx,)),
        dma((3 if layered else n_gx, chunks)),
        dma((3, chunks)),
        dma((LAYERS if layered else n_gx, chunks)),
        dma((2, chunks)),
        dma((2, chunks)),
        dma((2, chunks)),
    ]
    columns = source_column.reshape(-1)
    return pl.pallas_call(
        functools.partial(kernel, n_gy, n_gx, height, across),
        out_shape=jax.ShapeDtypeStruct((3, height, across, planes), f32),
        in_specs=[vmem, vmem, pl.BlockSpec(memory_space=pltpu.SMEM)],
        out_specs=vmem,
        scratch_shapes=scratch,
        compiler_params=pltpu.CompilerParams(
            collective_id=0, has_side_effects=True, vmem_limit_bytes=40 * 1024 * 1024
        ),
    )(first_frame, second_frame, columns)


def solution(mesh):
    return jax.shard_map(
        functools.partial(body, mesh.shape["gy"], mesh.shape["gx"]),
        mesh=mesh,
        in_specs=(P("gy", "gx", None), P("gy", "gx", None), P("gy", "gx", None, None)),
        out_specs=P(None, "gy", "gx", None),
        check_vma=False,
    )
```

```python
import functools

import jax
import jax.numpy as jnp
from jax import lax
from jax.experimental import pallas as pl
from jax.experimental.pallas import tpu as pltpu
from jax.sharding import PartitionSpec as P

BRICK = 32
LEVELS = 4
TIKHONOV = 0.05
CONTRAST = 0.5
RELAXATION = 0.8
FLOOR = 1.0
LANES = 128
PAD = 8
ROWS = 4
LAYERS = 4
BUFFERS = (4, 6, 6, 3)
AHEAD = 2
CELLS = 16
MESH = pl.DeviceIdType.MESH


def dot(a, b):
    return jnp.dot(a, b, preferred_element_type=jnp.float32)


def two_terms(x, axis):
    high = x.astype(jnp.bfloat16).astype(jnp.float32)
    return jnp.concatenate([high, x - high], axis=axis).astype(jnp.bfloat16)


def solve_three(t, diagonal, f):
    aa = t[0] + diagonal
    ab, ac, bc = t[1], t[2], t[4]
    bb = t[3] + diagonal
    cc = t[5] + diagonal
    c_aa = bb * cc - bc * bc
    c_ab = ac * bc - ab * cc
    c_ac = ab * bc - ac * bb
    c_bb = aa * cc - ac * ac
    c_bc = ab * ac - aa * bc
    c_cc = aa * bb - ab * ab
    inverse = 1.0 / (aa * c_aa + ab * c_ab + ac * c_ac)
    return (
        (c_aa * f[0] + c_ab * f[1] + c_ac * f[2]) * inverse,
        (c_ab * f[0] + c_bb * f[1] + c_bc * f[2]) * inverse,
        (c_ac * f[0] + c_bc * f[1] + c_cc * f[2]) * inverse,
    )


def apply_three(t, u):
    return (
        t[0] * u[0] + t[1] * u[1] + t[2] * u[2],
        t[1] * u[0] + t[3] * u[1] + t[4] * u[2],
        t[2] * u[0] + t[4] * u[1] + t[5] * u[2],
    )


def kernel(n_gy, n_gx, height, across, *refs):
    given, columns, out = refs[:3], refs[-1], refs[3]
    first, second = refs[-3:-1]
    refs = refs[:-3]
    cols, packets_in, packets_out, avg, avg_stage, avg_halo = refs[4:10]
    refs = refs[2:]
    moved = refs[8]
    tensors = (None, *refs[9:12])
    sources = (None, *refs[12:15])
    refs = refs[:15] + (None,) + refs[15:]
    iterates = refs[16:20]
    stages = refs[20:24]
    halos = refs[24:28]
    residues = refs[28:31]
    halo_send, halo_recv, avg_send, avg_recv, own_sem = refs[31:36]
    mine, table, picks, table_send, table_recv = refs[36:41]
    own_send, packet_send, col_recv, packet_recv, edge_send, edge_recv, load_sem = refs[41:]
    my_y, my_x = lax.axis_index("gy"), lax.axis_index("gx")
    bases = [sum(BUFFERS[:l]) * 4 for l in range(LEVELS)]
    hs = [height >> l for l in range(LEVELS)]
    ws = [across >> l for l in range(LEVELS)]
    wqs = [max(w, 8) for w in ws]

    loads = [
        pltpu.make_async_copy(source, target, load_sem.at[k])
        for k, (source, target) in enumerate(zip(given, (first, second, columns)))
    ]
    for load in loads:
        load.start()
    avg[0] = jnp.zeros(avg.shape[1:], jnp.float32)
    avg[height + 1] = jnp.zeros(avg.shape[1:], jnp.float32)
    avg_halo[...] = jnp.zeros(avg_halo.shape, jnp.float32)

    has_up, has_down = my_y > 0, my_y < n_gy - 1
    has_left, has_right = my_x > 0, my_x < n_gx - 1
    up, down = (jnp.maximum(my_y - 1, 0), my_x), (jnp.minimum(my_y + 1, n_gy - 1), my_x)
    left, right = (my_y, jnp.maximum(my_x - 1, 0)), (my_y, jnp.minimum(my_x + 1, n_gx - 1))

    barrier = pltpu.get_barrier_semaphore()
    for step in range(1, n_gx):
        pl.semaphore_signal(
            barrier, inc=1, device_id=(my_y, lax.rem(my_x + step, n_gx)), device_id_type=MESH
        )
    for present, device in ((has_up, up), (has_down, down)):

        @pl.when(present)
        def _(device=device):
            pl.semaphore_signal(barrier, inc=1, device_id=device, device_id_type=MESH)

    peers = n_gx - 1 + jnp.where(has_up, 1, 0) + jnp.where(has_down, 1, 0)
    pl.semaphore_wait(barrier, peers)
    for load in loads:
        load.wait()

    def to_peer(step, source, target, send, recv):
        return pltpu.make_async_remote_copy(
            src_ref=source,
            dst_ref=target,
            send_sem=send.at[step],
            recv_sem=recv.at[step],
            device_id=(my_y, lax.rem(my_x + step, n_gx)),
            device_id_type=MESH,
        )

    lane = lax.broadcasted_iota(jnp.int32, (8, LANES), 1)
    sub = lax.broadcasted_iota(jnp.int32, (8, LANES), 0)
    group = lax.broadcasted_iota(jnp.int32, (1, LANES), 1) // BRICK
    bricks = columns.shape[0]
    chunks = height // ROWS

    def ones(condition):
        return jnp.where(condition, 1.0, 0.0).astype(jnp.float32)

    def flag(condition):
        return jnp.where(condition, 1.0, 0.0).astype(jnp.float32)

    def remote(source, target, send, recv, device):
        return pltpu.make_async_remote_copy(
            src_ref=source,
            dst_ref=target,
            send_sem=send,
            recv_sem=recv,
            device_id=device,
            device_id_type=MESH,
        )

    def start_all(parts):
        for present, copy, _ in parts:

            @pl.when(present)
            def _(copy=copy):
                copy.start()

    def wait_all(parts):
        for present, copy, opposite in parts:

            @pl.when(present)
            def _(copy=copy, opposite=opposite):
                copy.wait_send()
                opposite.wait_recv()

    def rows_of(c):
        return pl.ds(c * ROWS, ROWS)

    def chunk_copy(source, target, send, recv, device):
        return remote(source, target, send, recv, device)

    layered = n_gx == 2 * LAYERS
    z, x = my_x // 2, my_x % 2
    inner = (z > 0) & (z < LAYERS - 1)
    ending = jnp.logical_not(inner)
    near = jnp.where(z == 0, 1, jnp.where(z == LAYERS - 1, LAYERS - 2, LAYERS - 1 - z))
    far = LAYERS - 1 - near
    end = jnp.where(z <= 1, 0, LAYERS - 1)

    def own_copies(c):
        rows = second.at[rows_of(c)]
        if not layered:
            return [
                (
                    None,
                    remote(
                        rows,
                        cols.at[my_x, rows_of(c)],
                        own_send.at[step, c],
                        col_recv.at[step, c],
                        (my_y, lax.rem(my_x + step, n_gx)),
                    ),
                )
                for step in range(1, n_gx)
            ]
        land = cols.at[z, rows_of(c)]
        return [
            (ending, remote(rows, land, own_send.at[1, c], col_recv.at[z, c], (my_y, 2 * far + x))),
            (None, remote(rows, land, own_send.at[0, c], col_recv.at[z, c], (my_y, 2 * near + x))),
            (ending, remote(rows, land, own_send.at[2, c], col_recv.at[z, c], (my_y, 2 * z + 1 - x))),
        ]

    def column_arrival(k, c):
        return remote(
            second.at[rows_of(c)],
            cols.at[k, rows_of(c)],
            own_send.at[0, c],
            col_recv.at[k, c],
            (my_y, lax.rem(my_x + 1, n_gx)),
        )

    def packet_copies(c):
        targets = [(my_y, 2 * end), (my_y, 2 * end + 1), (my_y, 2 * z + 1 - x)]
        return [
            remote(
                packets_out.at[i, rows_of(c)],
                packets_in.at[x, rows_of(c)],
                packet_send.at[i, c],
                packet_recv.at[x, c],
                device,
            )
            for i, device in enumerate(targets)
        ]

    def packet_arrival(k, c):
        return remote(
            packets_out.at[0, rows_of(c)],
            packets_in.at[k, rows_of(c)],
            packet_send.at[0, c],
            packet_recv.at[k, c],
            (my_y, lax.rem(my_x + 1, n_gx)),
        )

    def guarded(condition, act):
        if condition is None:
            act()
        else:
            pl.when(condition)(act)

    def send_own(t, carry):
        for condition, copy in own_copies((t + chunks - 1) % chunks):
            guarded(condition, copy.start)
        return carry

    for p in range(8):
        mine[pl.ds(p, 1)] = jnp.full((1, LANES), columns[min(p, bricks - 1)], jnp.int32)
    if layered:
        copies = [
            to_peer(step, mine, table.at[my_x], table_send, table_recv) for step in range(1, n_gx)
        ]
        for copy in copies:
            copy.start()
        keep = pltpu.make_async_copy(second, cols.at[z], own_sem)
        pl.when(inner)(keep.start)
    lax.fori_loop(0, AHEAD, send_own, 0)
    for l in range(LEVELS):
        u, w, wq, h = iterates[l], ws[l], wqs[l], hs[l]
        for b in range(BUFFERS[l]):
            zero_row = jnp.zeros((3, wq + 2 * PAD, LANES), jnp.float32)
            u[b, :, 0] = zero_row
            u[b, :, h + 1] = zero_row
            halos[l][b] = jnp.zeros(halos[l].shape[1:], jnp.float32)
    iterates[LEVELS - 1][...] = jnp.zeros(iterates[LEVELS - 1].shape, jnp.float32)

    def wanted(entry):
        value = entry(0)
        for p in range(1, bricks):
            value = jnp.where(group == p, entry(p), value)
        return value

    picks[pl.ds(3, 1)] = wanted(lambda p: mine[pl.ds(p, 1)])
    if layered:
        pl.when(inner)(keep.wait)
        for copy in copies:
            copy.wait()
        for i, device in enumerate((2 * end, 2 * end + 1, 2 * z + 1 - x)):
            picks[pl.ds(i, 1)] = wanted(lambda p: table[device, pl.ds(p, 1)])

    def pick_of(i):
        return jnp.broadcast_to(picks[pl.ds(i, 1)], (across, LANES))

    def by_layer(values, layers):
        value = values[0]
        for k in range(1, LAYERS):
            value = jnp.where(layers == k, values[k], value)
        return value

    def forward(c):
        for k in range(LAYERS):

            @pl.when(z != k)
            def _(k=k):
                column_arrival(k, c).wait_recv()

        layers = [pick_of(i) // 2 for i in range(3)]
        for row in range(ROWS):
            r = c * ROWS + row
            values = [cols[k, r] for k in range(LAYERS)]
            for i in range(3):
                packets_out[i, r] = by_layer(values, layers[i])
        for copy in packet_copies(c):
            copy.start()

    def edges(c):
        return [
            (
                has_left,
                remote(avg_stage.at[c, 0], avg_halo.at[c, 1], edge_send.at[0, c], edge_recv.at[0, c], left),
                remote(avg_stage.at[c, 1], avg_halo.at[c, 0], edge_send.at[1, c], edge_recv.at[1, c], right),
            ),
            (
                has_right,
                remote(avg_stage.at[c, 1], avg_halo.at[c, 0], edge_send.at[1, c], edge_recv.at[1, c], right),
                remote(avg_stage.at[c, 0], avg_halo.at[c, 1], edge_send.at[0, c], edge_recv.at[0, c], left),
            ),
        ]

    def average(c, row, value):
        r = c * ROWS + row
        value = 0.5 * (first[r] + value)
        avg[r + 1, pl.ds(PAD, across)] = value
        avg_stage[c, 0, pl.ds(row, 1)] = value[0:1]
        avg_stage[c, 1, pl.ds(row, 1)] = value[across - 1 : across]

    def averages(c):
        pick = pick_of(3)
        if not layered:
            for step in range(1, n_gx):
                remote(
                    second.at[rows_of(c)],
                    cols.at[lax.rem(my_x - step + n_gx, n_gx), rows_of(c)],
                    own_send.at[step, c],
                    col_recv.at[step, c],
                    (my_y, lax.rem(my_x + step, n_gx)),
                ).wait_recv()
            for row in range(ROWS):
                value = second[c * ROWS + row]
                for step in range(1, n_gx):
                    k = lax.rem(my_x + step, n_gx)
                    value = jnp.where(pick == k, cols[k, c * ROWS + row], value)
                average(c, row, value)
        else:
            layer, side = pick // 2, pick % 2

            @pl.when(inner)
            def _():
                packet_arrival(1 - x, c).wait_recv()
                for row in range(ROWS):
                    r = c * ROWS + row
                    value = by_layer([cols[k, r] for k in range(LAYERS)], layer)
                    average(c, row, jnp.where(side == x, value, packets_in[1 - x, r]))

            @pl.when(ending)
            def _():
                column_arrival(z, c).wait_recv()
                for k in range(2):
                    packet_arrival(k, c).wait_recv()
                for row in range(ROWS):
                    r = c * ROWS + row
                    value = jnp.where(side == 0, packets_in[0, r], packets_in[1, r])
                    same = jnp.where(side == x, second[r], cols[z, r])
                    average(c, row, jnp.where(layer == z, same, value))

        for present, copy, _ in edges(c):
            pl.when(present)(copy.start)

    def place_average(c):
        for present, _, opposite in edges(c):
            pl.when(present)(opposite.wait_recv)
        for row in range(ROWS):
            r = c * ROWS + row
            avg[r + 1, pl.ds(PAD - 1, 1)] = avg_halo[c, 0, pl.ds(row, 1)]
            avg[r + 1, pl.ds(PAD + across, 1)] = avg_halo[c, 1, pl.ds(row, 1)]

    to_up = remote(avg.at[1], avg.at[height + 1], avg_send.at[0], avg_recv.at[0], up)
    to_down = remote(avg.at[height], avg.at[0], avg_send.at[1], avg_recv.at[1], down)
    row_parts = [(has_up, to_up, to_down), (has_down, to_down, to_up)]

    def row_flags(l, r):
        h = hs[l]
        at = my_y * h + r
        return flag(at > 0), flag(at < n_gy * h - 1)

    def masks_of(l):
        w, planes = ws[l], LANES >> l
        first_column = ones((sub > 0) | has_left)
        last_column = ones((sub != (w - 1) % 8) | has_right)
        below = ones((lane > 0) & (lane < planes))
        above = ones(lane < planes - 1)
        return first_column, last_column, below, above

    masks = [masks_of(l) for l in range(LEVELS)]

    def exchange(l, b):
        h, wq = hs[l], wqs[l]
        u, stage, halo = iterates[l], stages[l], halos[l]
        base = bases[l] + 4 * b
        inner = pl.ds(PAD, wq)
        send = [halo_send.at[base + d] for d in range(4)]
        recv = [halo_recv.at[base + d] for d in range(4)]
        to_up = remote(u.at[b, :, 1, inner], u.at[b, :, h + 1, inner], send[0], recv[0], up)
        to_down = remote(u.at[b, :, h, inner], u.at[b, :, 0, inner], send[1], recv[1], down)
        to_left = remote(stage.at[b, 0], halo.at[b, 1], send[2], recv[2], left)
        to_right = remote(stage.at[b, 1], halo.at[b, 0], send[3], recv[3], right)
        return [
            (has_up, to_up, to_down),
            (has_down, to_down, to_up),
            (has_left, to_left, to_right),
            (has_right, to_right, to_left),
        ]

    def place_halo(l, b, r):
        u, halo, w = iterates[l], halos[l], ws[l]
        for i in range(3):
            u[b, i, r + 1, pl.ds(PAD - 1, 1)] = halo[b, 0, i, pl.ds(r, 1)]
            u[b, i, r + 1, pl.ds(PAD + w, 1)] = halo[b, 1, i, pl.ds(r, 1)]

    def store_chunk(l, b, r, j, new):
        u, stage, w = iterates[l], stages[l], ws[l]
        for i in range(3):
            u[b, i, r + 1, pl.ds(PAD + 8 * j, 8)] = new[i]
            if j == 0:
                stage[b, 0, i, pl.ds(r, 1)] = new[i][0:1]
            if j == wqs[l] // 8 - 1:
                k = (w - 1) % 8
                stage[b, 1, i, pl.ds(r, 1)] = new[i][k : k + 1]

    last_sub = sub == 7

    def sweep(l, b, start, count, js, group, compute, store):
        u = iterates[l]
        first_column, last_column, below, above = masks[l]
        end = wqs[l] // 8 - 1
        scale = 0.25**l / (CONTRAST * CONTRAST) / (4.0 if l == 0 else 1.0)

        def at(r, j, shift=0):
            return [u[b, i, r + 1, pl.ds(PAD + 8 * j + shift, 8)] for i in range(3)]

        def face(before, after, mask):
            change = [q - p for p, q in zip(before, after)]
            spread = change[0] * change[0] + change[1] * change[1] + change[2] * change[2]
            if scale != 1.0:
                spread = spread * scale
            weight = lax.rsqrt(1.0 + spread)
            if mask is not None:
                weight = weight * mask
            return [weight * c for c in change] + [weight]

        def row(r, carry):
            flags = row_flags(l, r)
            results, lower, previous = [], [], None
            for n, j in enumerate(js):
                center = at(r, j)
                down = face(center, at(r + 1, j), flags[1])
                lower.append(down)
                side = face(center, [pltpu.roll(c, LANES - 1, 1) for c in center], above)
                right = face(center, at(r, j, 1), last_column if j == end else None)
                if j - 1 in js:
                    left = [
                        pltpu.roll(jnp.where(last_sub, p, q), 1, 0) for p, q in zip(previous, right)
                    ]
                else:
                    left = face(at(r, j, -1), center, first_column if j == 0 else None)
                previous = right
                back = face([pltpu.roll(c, 1, 1) for c in center], center, below)
                up = carry[n]
                flux = [
                    (down[i] - up[i]) + (side[i] - back[i]) + (right[i] - left[i]) for i in range(3)
                ]
                total = (down[3] + up[3]) + (side[3] + back[3]) + (right[3] + left[3])
                results.append(compute(r, j, center, flux, total))
            return results, lower

        def step(k, carry):
            base = start + k * group
            if 0 in js or end in js:
                for n in range(group):
                    place_halo(l, b, base + n)
            done = []
            for n in range(group):
                results, carry = row(base + n, carry)
                done.append(results)
            for n in range(group):
                for j, result in zip(js, done[n]):
                    store(base + n, j, result)
            return carry

        flags = row_flags(l, start)
        carry = [face(at(start - 1, j), at(start, j), flags[0]) for j in js]
        if count == group:
            step(0, carry)
        else:
            lax.fori_loop(0, count // group, step, carry)

    def part(l, b, which, compute, store):
        h = hs[l]
        every = tuple(range(wqs[l] // 8))
        if which == "all":
            sweep(l, b, 0, h, every, min(h, max(1, CELLS // len(every))), compute, store)
        elif which == "edge":
            sweep(l, b, 0, h, (every[0], every[-1]), CELLS // 2, compute, store)
            for r in (0, h - 1):
                sweep(l, b, r, 1, every[1:-1], 1, compute, store)
        else:
            sweep(l, b, 1, h - 2, every[1:-1], 6, compute, store)

    def motion_of(r, j):
        return [moved[k, r, pl.ds(8 * j, 8)] for k in range(5)]

    def tensor_of(l, r, j):
        return [tensors[l][k, r, pl.ds(8 * j, 8)] for k in range(6)]

    def source_of(l, r, j):
        return [sources[l][k, r, pl.ds(8 * j, 8)] for k in range(3)]

    def relax(l, b, target, which="all"):
        coupling = 0.25**l
        gain = 0.5 if target is None else 1.0

        def compute(r, j, center, flux, total):
            if l == 0:
                h0, h1, h2, time, hh = motion_of(r, j)
                around = [q + total * c for q, c in zip(flux, center)]
                diagonal = TIKHONOV + total
                widened = diagonal + hh
                common = h0 * around[0] + h1 * around[1] + h2 * around[2] + diagonal * time
                inverse = (gain * RELAXATION) / (diagonal * widened)
                keep = gain * (1.0 - RELAXATION)
                return [
                    keep * c + (q * widened - g * common) * inverse
                    for c, q, g in zip(center, around, (h0, h1, h2))
                ]
            solved = solve_three(
                tensor_of(l, r, j),
                TIKHONOV + coupling * total,
                [
                    f + coupling * (q + total * c)
                    for f, q, c in zip(source_of(l, r, j), flux, center)
                ],
            )
            return [c + RELAXATION * (s - c) for c, s in zip(center, solved)]

        def store(r, j, new):
            if target is None:
                for i in range(3):
                    out[i, r, pl.ds(8 * j, 8)] = new[i]
            else:
                store_chunk(l, target, r, j, new)

        part(l, b, which, compute, store)

    def residue(l, b, which="all"):
        coupling = 0.25**l

        def compute(r, j, center, flux, total):
            if l == 0:
                h0, h1, h2, time, _ = motion_of(r, j)
                common = h0 * center[0] + h1 * center[1] + h2 * center[2] + time
                return [
                    q - TIKHONOV * c - g * common for c, q, g in zip(center, flux, (h0, h1, h2))
                ]
            value = apply_three(tensor_of(l, r, j), center)
            return [
                f + coupling * q - TIKHONOV * c - a
                for f, q, c, a in zip(source_of(l, r, j), flux, center, value)
            ]

        def store(r, j, new):
            for i in range(3):
                residues[l][i, r, pl.ds(8 * j, 8)] = new[i]

        part(l, b, which, compute, store)

    def enter(l):
        coupling = 0.25**l

        def compute(r, j, center, flux, total):
            tensor, given = tensor_of(l, r, j), source_of(l, r, j)
            value = apply_three(tensor, center)
            source = [
                f + a + TIKHONOV * c - coupling * q
                for f, a, c, q in zip(given, value, center, flux)
            ]
            solved = solve_three(tensor, TIKHONOV + coupling * total, given)
            return source, [c + RELAXATION * s for c, s in zip(center, solved)]

        def store(r, j, result):
            source, new = result
            for i in range(3):
                sources[l][i, r, pl.ds(8 * j, 8)] = source[i]
            store_chunk(l, 1, r, j, new)

        part(l, 0, "all", compute, store)

    fine_lane = lax.broadcasted_iota(jnp.int32, (LANES, LANES), 0)
    coarse_lane = lax.broadcasted_iota(jnp.int32, (LANES, LANES), 1)
    halving = ones(fine_lane // 2 == coarse_lane)
    squeeze = jnp.concatenate([halving, halving], axis=0).astype(jnp.bfloat16)
    doubling = ones(coarse_lane // 2 == fine_lane)
    spread = jnp.concatenate([doubling, doubling], axis=0).astype(jnp.bfloat16)

    def corners(j, k, rest):
        return [
            (row, pl.ds(rest + 16 * j + parity, k, stride=2)) for row in range(2) for parity in range(2)
        ]

    def filled(x):
        if x.shape[0] == 8:
            return x
        return jnp.concatenate([x, jnp.zeros((8 - x.shape[0], LANES), jnp.float32)], axis=0)

    def shrink(l, rows, sums, factor, store):
        chunks = wqs[l + 1] // 8
        pieces = [[sums(r, j) for j in range(chunks)] for r in rows]
        flat = [filled(x) for of_row in pieces for of_chunk in of_row for x in of_chunk]
        y = dot(two_terms(jnp.concatenate(flat, axis=0), 1), squeeze) * factor
        at = 0
        for r in rows:
            for j in range(chunks):
                for i in range(len(pieces[0][0])):
                    store(r, j, i, y[8 * at : 8 * at + 8])
                    at += 1

    def summed(load, cells):
        values = [load(row, columns) for row, columns in cells]
        return (values[0] + values[1]) + (values[2] + values[3])

    def all_rows(l, work):
        group = min(4, hs[l])

        def step(k, carry):
            work([k * group + n for n in range(group)])
            return carry

        if hs[l] == group:
            step(0, 0)
        else:
            lax.fori_loop(0, hs[l] // group, step, 0)

    def shrink_iterate(l, b):
        u = iterates[l]
        coarse, stage, w = iterates[l + 1], stages[l + 1], ws[l + 1]
        k = min(8, w)

        def sums(r, j):
            cells = corners(j, k, PAD)
            return [
                summed(lambda row, columns, i=i: u[b, i, 2 * r + row + 1, columns], cells)
                for i in range(3)
            ]

        def store(r, j, i, y):
            coarse[0, i, r + 1, pl.ds(PAD + 8 * j, 8)] = y
            if j == 0:
                stage[0, 0, i, pl.ds(r, 1)] = y[0:1]
            if j == wqs[l + 1] // 8 - 1:
                n = (w - 1) % 8
                stage[0, 1, i, pl.ds(r, 1)] = y[n : n + 1]

        factor = 0.0625 if l == 0 else 0.125
        all_rows(l + 1, lambda rows: shrink(l, rows, sums, factor, store))

    def shrink_array(l, fine, coarse, factor):
        k = min(8, ws[l + 1])

        def sums(r, j):
            cells = corners(j, k, 0)
            return [
                summed(lambda row, columns, i=i: fine[i, 2 * r + row, columns], cells)
                for i in range(fine.shape[0])
            ]

        def store(r, j, i, y):
            coarse[i, r, pl.ds(8 * j, 8)] = y

        all_rows(l + 1, lambda rows: shrink(l, rows, sums, factor, store))

    def shrink_motion(rows):
        def sums(r, j):
            values = None
            for row, columns in corners(j, min(8, ws[1]), 0):
                h0, h1, h2 = [moved[k, 2 * r + row, columns] for k in range(3)]
                terms = [h0 * h0, h0 * h1, h0 * h2, h1 * h1, h1 * h2, h2 * h2]
                values = terms if values is None else [v + t for v, t in zip(values, terms)]
            return values

        def store(r, j, i, y):
            tensors[1][i, r, pl.ds(8 * j, 8)] = y

        shrink(0, rows, sums, 0.125, store)

    def grow(l, b, solved, target, arriving):
        wc, hc, h = wqs[l + 1], hs[l + 1], hs[l]
        kc, kr = min(8, ws[l + 1]), min(8, hc)
        u, coarse = iterates[l], iterates[l + 1]

        def spread_out(x):
            y = dot(two_terms(x, 1), spread)
            return 2.0 * y if l == 0 else y

        def correction(r):
            inner = pl.ds(PAD, wc)
            return (coarse[solved, :, r + 1, inner] - coarse[0, :, r + 1, inner]).reshape(3 * wc, LANES)

        def add(y, first_row, targets):
            for i in range(3):
                for j in range(wc // 8):
                    at = first_row + i * wc + 8 * j
                    piece = y[at : at + kc]
                    for row in targets:
                        for parity in range(2):
                            columns = pl.ds(PAD + 16 * j + parity, kc, stride=2)
                            u[target, i, row, columns] = u[b, i, row, columns] + piece

        def work(rows):
            y = spread_out(jnp.concatenate([correction(r) for r in rows], axis=0))
            for n, r in enumerate(rows):
                add(y, n * 3 * wc, (2 * r + 1, 2 * r + 2))

        all_rows(l + 1, work)
        wait_all(arriving)
        y = spread_out(jnp.concatenate([correction(-1), correction(hc)], axis=0))
        add(y, 0, (0,))
        add(y, 3 * wc, (h + 1,))
        hq = max(8, hc)
        halo, coarse_halo = halos[l], halos[l + 1]
        y = spread_out((coarse_halo[solved] - coarse_halo[0]).reshape(6 * hq, LANES))
        for side in range(2):
            for i in range(3):
                for j in range(hq // 8):
                    at = (side * 3 + i) * hq + 8 * j
                    for parity in range(2):
                        rows = pl.ds(16 * j + parity, kr, stride=2)
                        halo[target, side, i, rows] = halo[b, side, i, rows] + y[at : at + kr]

    first_column, last_column, below, above = masks[0]

    def motion(r):
        flags = row_flags(0, r)
        for j in range(across // 8):
            s = PAD + 8 * j
            diffs, sums = [], []
            for shift in (-1, 0, 1):
                lower = avg[r, pl.ds(s + shift, 8)]
                middle = avg[r + 1, pl.ds(s + shift, 8)]
                upper = avg[r + 2, pl.ds(s + shift, 8)]
                diffs.append(0.5 * (upper - lower))
                sums.append(0.25 * (lower + 2.0 * middle + upper))
            along_rows = 0.25 * (diffs[0] + 2.0 * diffs[1] + diffs[2])
            along_cols = 0.5 * (sums[2] - sums[0])
            along_planes = 0.25 * (sums[0] + 2.0 * sums[1] + sums[2])

            def beside(x):
                return pltpu.roll(x, 1, 1) * below, pltpu.roll(x, LANES - 1, 1) * above

            def smooth(x):
                lower, upper = beside(x)
                return 0.25 * (lower + 2.0 * x + upper)

            g0, g1 = smooth(along_rows), smooth(along_cols)
            lower, upper = beside(along_planes)
            g2 = 0.5 * (upper - lower)
            square = g0 * g0 + g1 * g1 + g2 * g2
            root = lax.rsqrt(square + FLOOR)
            h = [g0 * root, g1 * root, g2 * root]
            hh = square * root * root
            base = first[r, pl.ds(8 * j, 8)]
            time = (4.0 * root) * (avg[r + 1, pl.ds(s, 8)] - base)
            for k, value in enumerate((*h, time, hh)):
                moved[k, r, pl.ds(8 * j, 8)] = value
            total = below + above + (flags[0] + flags[1])
            total = total + (first_column if j == 0 else 1.0)
            total = total + (last_column if j == across // 8 - 1 else 1.0)
            length = time * (-RELAXATION / (TIKHONOV + total + hh))
            store_chunk(0, 0, r, j, [g * length for g in h])

    def shrink_block(m):
        shrink_motion([m * (ROWS // 2) + k for k in range(ROWS // 2)])

    def motion_block(m):
        for row in range(ROWS):
            motion(m * ROWS + row)
        shrink_block(m)

    def gather_step(s, carry):
        @pl.when(s + AHEAD < chunks)
        def _():
            send_own(s + AHEAD, 0)

        def chunk_at(t):
            return (t + chunks - 1) % chunks

        if layered:
            pl.when(inner & (s < chunks))(lambda: forward(chunk_at(s)))
        pl.when((s >= 1) & (s <= chunks))(lambda: averages(chunk_at(s - 1)))
        pl.when(s >= 2)(lambda: place_average(chunk_at(s - 2)))
        pl.when(s == 3)(lambda: start_all(row_parts))
        pl.when(s >= 5)(lambda: motion_block(s - 4))

        @pl.when(s == chunks)
        def _():
            wait_all(row_parts)
            motion_block(0)
            for row in range(1, ROWS):
                motion(height - ROWS + row)

        return carry

    lax.fori_loop(0, chunks + 2, gather_step, 0)
    for row in range(ROWS):
        motion((chunks - 2) * ROWS + row)
    motion(height - ROWS)
    arriving = exchange(0, 0)
    start_all(arriving)
    shrink_block(chunks - 2)
    shrink_block(chunks - 1)

    def finish_sends(c, carry):
        for condition, copy in own_copies(c):
            guarded(condition, copy.wait_send)
        if layered:
            for copy in packet_copies(c):
                pl.when(inner)(copy.wait_send)
        for present, copy, _ in edges(c):
            pl.when(present)(copy.wait_send)
        return carry

    lax.fori_loop(0, chunks, finish_sends, 0)
    for l in range(1, LEVELS - 1):
        shrink_array(l, tensors[l], tensors[l + 1], 0.125)
    relax(0, 0, 1, "inner")
    wait_all(arriving)
    relax(0, 0, 1, "edge")
    for l in range(LEVELS - 1):
        b = 1 if l == 0 else 2
        current = exchange(l, b)
        start_all(current)
        shrink_iterate(l, b)
        following = exchange(l + 1, 0)
        start_all(following)
        if l == 0:
            residue(l, b, "inner")
        wait_all(current)
        residue(l, b, "edge" if l == 0 else "all")
        shrink_array(l, residues[l], sources[l + 1], 0.0625 if l == 0 else 0.125)
        wait_all(following)
        enter(l + 1)
        current = exchange(l + 1, 1)
        start_all(current)
        wait_all(current)
        relax(l + 1, 1, 2)
    for l in range(LEVELS - 2, -1, -1):
        b = 1 if l == 0 else 2
        solved = 2 if l == LEVELS - 2 else 5
        arriving = exchange(l + 1, solved)
        start_all(arriving)
        grow(l, b, solved, b + 1, arriving)
        if l > 0:
            relax(l, b + 1, b + 2)
            current = exchange(l, b + 2)
            start_all(current)
            wait_all(current)
            relax(l, b + 2, b + 3)
    relax(0, 2, 3, "edge")
    current = exchange(0, 3)
    start_all(current)
    relax(0, 2, 3, "inner")
    relax(0, 3, None, "inner")
    wait_all(current)
    relax(0, 3, None, "edge")


def body(n_gy, n_gx, first_frame, second_frame, source_column):
    height, across, planes = first_frame.shape
    f32 = jnp.float32
    hs = [height >> l for l in range(LEVELS)]
    wqs = [max(across >> l, 8) for l in range(LEVELS)]
    hqs = [max(h, 8) for h in hs]
    total = sum(BUFFERS) * 4
    vmem = pl.BlockSpec(memory_space=pltpu.VMEM)
    chunks = height // ROWS
    layered = n_gx == 2 * LAYERS
    volume = (height, across, LANES)
    scratch = [
        pltpu.VMEM((LAYERS if layered else n_gx, *volume), f32),
        pltpu.VMEM((2, *volume) if layered else (2, 8, LANES), f32),
        pltpu.VMEM((3, *volume) if layered else (3, 8, LANES), f32),
        pltpu.VMEM((height + 2, across + 2 * PAD, LANES), f32),
        pltpu.VMEM((chunks, 2, 8, LANES), f32),
        pltpu.VMEM((chunks, 2, 8, LANES), f32),
    ]
    scratch += [pltpu.VMEM((6 if l else 5, hs[l], wqs[l], LANES), f32) for l in range(LEVELS)]
    scratch += [pltpu.VMEM((3, hs[l], wqs[l], LANES), f32) for l in range(1, LEVELS)]
    scratch += [
        pltpu.VMEM((BUFFERS[l], 3, hs[l] + 2, wqs[l] + 2 * PAD, LANES), f32)
        for l in range(LEVELS)
    ]
    scratch += [pltpu.VMEM((BUFFERS[l], 2, 3, hqs[l], LANES), f32) for l in range(LEVELS)] * 2
    scratch += [pltpu.VMEM((3, hs[l], wqs[l], LANES), f32) for l in range(LEVELS - 1)]
    dma = pltpu.SemaphoreType.DMA
    scratch += [dma((total,)), dma((total,)), dma((2,)), dma((2,)), dma]
    scratch += [
        pltpu.VMEM((8, LANES), jnp.int32),
        pltpu.VMEM((n_gx, 8, LANES), jnp.int32),
        pltpu.VMEM((8, LANES), jnp.int32),
        dma((n_gx,)),
        dma((n_gx,)),
        dma((3 if layered else n_gx, chunks)),
        dma((3, chunks)),
        dma((LAYERS if layered else n_gx, chunks)),
        dma((2, chunks)),
        dma((2, chunks)),
        dma((2, chunks)),
        dma((3,)),
        pltpu.VMEM(volume, f32),
        pltpu.VMEM(volume, f32),
        pltpu.SMEM((source_column.size,), jnp.int32),
    ]
    columns = source_column.reshape(-1)
    return pl.pallas_call(
        functools.partial(kernel, n_gy, n_gx, height, across),
        out_shape=jax.ShapeDtypeStruct((3, height, across, planes), f32),
        in_specs=[pl.BlockSpec(memory_space=pltpu.HBM)] * 3,
        out_specs=vmem,
        scratch_shapes=scratch,
        compiler_params=pltpu.CompilerParams(
            collective_id=0, has_side_effects=True, vmem_limit_bytes=40 * 1024 * 1024
        ),
    )(*(pltpu.with_memory_space_constraint(x, pltpu.HBM) for x in (first_frame, second_frame, columns)))


def solution(mesh):
    return jax.shard_map(
        functools.partial(body, mesh.shape["gy"], mesh.shape["gx"]),
        mesh=mesh,
        in_specs=(P("gy", "gx", None), P("gy", "gx", None), P("gy", "gx", None, None)),
        out_specs=P(None, "gy", "gx", None),
        check_vma=False,
    )
```

```python
import functools

import jax
import jax.numpy as jnp
from jax import lax
from jax.experimental import pallas as pl
from jax.experimental.pallas import tpu as pltpu
from jax.sharding import PartitionSpec as P

BRICK = 32
LEVELS = 4
TIKHONOV = 0.05
CONTRAST = 0.5
RELAXATION = 0.8
FLOOR = 1.0
LANES = 128
PAD = 8
ROWS = 4
LAYERS = 4
BUFFERS = (4, 6, 6, 3)
AHEAD = 2
CELLS = 16
MESH = pl.DeviceIdType.MESH


def dot(a, b):
    return jnp.dot(a, b, preferred_element_type=jnp.float32)


def two_terms(x, axis):
    high = x.astype(jnp.bfloat16).astype(jnp.float32)
    return jnp.concatenate([high, x - high], axis=axis).astype(jnp.bfloat16)


def solve_three(t, diagonal, f):
    aa = t[0] + diagonal
    ab, ac, bc = t[1], t[2], t[4]
    bb = t[3] + diagonal
    cc = t[5] + diagonal
    c_aa = bb * cc - bc * bc
    c_ab = ac * bc - ab * cc
    c_ac = ab * bc - ac * bb
    c_bb = aa * cc - ac * ac
    c_bc = ab * ac - aa * bc
    c_cc = aa * bb - ab * ab
    inverse = 1.0 / (aa * c_aa + ab * c_ab + ac * c_ac)
    return (
        (c_aa * f[0] + c_ab * f[1] + c_ac * f[2]) * inverse,
        (c_ab * f[0] + c_bb * f[1] + c_bc * f[2]) * inverse,
        (c_ac * f[0] + c_bc * f[1] + c_cc * f[2]) * inverse,
    )


def apply_three(t, u):
    return (
        t[0] * u[0] + t[1] * u[1] + t[2] * u[2],
        t[1] * u[0] + t[3] * u[1] + t[4] * u[2],
        t[2] * u[0] + t[4] * u[1] + t[5] * u[2],
    )


def kernel(n_gy, n_gx, height, across, *refs):
    given, columns, out = refs[:3], refs[-1], refs[3]
    first, second = refs[-3:-1]
    refs = refs[:-3]
    cols, packets_in, packets_out, avg, avg_stage, avg_halo = refs[4:10]
    refs = refs[2:]
    moved = refs[8]
    tensors = (None, *refs[9:12])
    sources = (None, *refs[12:15])
    refs = refs[:15] + (None,) + refs[15:]
    iterates = refs[16:20]
    stages = refs[20:24]
    halos = refs[24:28]
    residues = refs[28:31]
    halo_send, halo_recv, avg_send, avg_recv, own_sem = refs[31:36]
    mine, table, picks, table_send, table_recv = refs[36:41]
    own_send, packet_send, col_recv, packet_recv, edge_send, edge_recv, load_sem = refs[41:]
    my_y, my_x = lax.axis_index("gy"), lax.axis_index("gx")
    bases = [sum(BUFFERS[:l]) * 4 for l in range(LEVELS)]
    hs = [height >> l for l in range(LEVELS)]
    ws = [across >> l for l in range(LEVELS)]
    wqs = [max(w, 8) for w in ws]

    loads = [
        pltpu.make_async_copy(source, target, load_sem.at[k])
        for k, (source, target) in enumerate(zip(given, (first, second, columns)))
    ]
    for load in loads:
        load.start()
    avg[0] = jnp.zeros(avg.shape[1:], jnp.float32)
    avg[height + 1] = jnp.zeros(avg.shape[1:], jnp.float32)
    avg_halo[...] = jnp.zeros(avg_halo.shape, jnp.float32)

    has_up, has_down = my_y > 0, my_y < n_gy - 1
    has_left, has_right = my_x > 0, my_x < n_gx - 1
    up, down = (jnp.maximum(my_y - 1, 0), my_x), (jnp.minimum(my_y + 1, n_gy - 1), my_x)
    left, right = (my_y, jnp.maximum(my_x - 1, 0)), (my_y, jnp.minimum(my_x + 1, n_gx - 1))

    barrier = pltpu.get_barrier_semaphore()
    for step in range(1, n_gx):
        pl.semaphore_signal(
            barrier, inc=1, device_id=(my_y, lax.rem(my_x + step, n_gx)), device_id_type=MESH
        )
    for present, device in ((has_up, up), (has_down, down)):

        @pl.when(present)
        def _(device=device):
            pl.semaphore_signal(barrier, inc=1, device_id=device, device_id_type=MESH)

    peers = n_gx - 1 + jnp.where(has_up, 1, 0) + jnp.where(has_down, 1, 0)
    pl.semaphore_wait(barrier, peers)
    for load in loads:
        load.wait()

    def to_peer(step, source, target, send, recv):
        return pltpu.make_async_remote_copy(
            src_ref=source,
            dst_ref=target,
            send_sem=send.at[step],
            recv_sem=recv.at[step],
            device_id=(my_y, lax.rem(my_x + step, n_gx)),
            device_id_type=MESH,
        )

    lane = lax.broadcasted_iota(jnp.int32, (8, LANES), 1)
    sub = lax.broadcasted_iota(jnp.int32, (8, LANES), 0)
    group = lax.broadcasted_iota(jnp.int32, (1, LANES), 1) // BRICK
    bricks = columns.shape[0]
    chunks = height // ROWS

    def ones(condition):
        return jnp.where(condition, 1.0, 0.0).astype(jnp.float32)

    def flag(condition):
        return jnp.where(condition, 1.0, 0.0).astype(jnp.float32)

    def remote(source, target, send, recv, device):
        return pltpu.make_async_remote_copy(
            src_ref=source,
            dst_ref=target,
            send_sem=send,
            recv_sem=recv,
            device_id=device,
            device_id_type=MESH,
        )

    def start_all(parts):
        for present, copy, _ in parts:

            @pl.when(present)
            def _(copy=copy):
                copy.start()

    def wait_all(parts):
        for present, copy, opposite in parts:

            @pl.when(present)
            def _(copy=copy, opposite=opposite):
                copy.wait_send()
                opposite.wait_recv()

    def rows_of(c):
        return pl.ds(c * ROWS, ROWS)

    def chunk_copy(source, target, send, recv, device):
        return remote(source, target, send, recv, device)

    layered = n_gx == 2 * LAYERS
    z, x = my_x // 2, my_x % 2
    inner = (z > 0) & (z < LAYERS - 1)
    ending = jnp.logical_not(inner)
    near = jnp.where(z == 0, 1, jnp.where(z == LAYERS - 1, LAYERS - 2, LAYERS - 1 - z))
    far = LAYERS - 1 - near
    end = jnp.where(z <= 1, 0, LAYERS - 1)

    def own_copies(c):
        rows = second.at[rows_of(c)]
        if not layered:
            return [
                (
                    None,
                    remote(
                        rows,
                        cols.at[my_x, rows_of(c)],
                        own_send.at[step, c],
                        col_recv.at[step, c],
                        (my_y, lax.rem(my_x + step, n_gx)),
                    ),
                )
                for step in range(1, n_gx)
            ]
        land = cols.at[z, rows_of(c)]
        return [
            (ending, remote(rows, land, own_send.at[1, c], col_recv.at[z, c], (my_y, 2 * far + x))),
            (None, remote(rows, land, own_send.at[0, c], col_recv.at[z, c], (my_y, 2 * near + x))),
            (ending, remote(rows, land, own_send.at[2, c], col_recv.at[z, c], (my_y, 2 * z + 1 - x))),
        ]

    def column_arrival(k, c):
        return remote(
            second.at[rows_of(c)],
            cols.at[k, rows_of(c)],
            own_send.at[0, c],
            col_recv.at[k, c],
            (my_y, lax.rem(my_x + 1, n_gx)),
        )

    def packet_copies(c):
        targets = [(my_y, 2 * end), (my_y, 2 * end + 1), (my_y, 2 * z + 1 - x)]
        return [
            remote(
                packets_out.at[i, rows_of(c)],
                packets_in.at[x, rows_of(c)],
                packet_send.at[i, c],
                packet_recv.at[x, c],
                device,
            )
            for i, device in enumerate(targets)
        ]

    def packet_arrival(k, c):
        return remote(
            packets_out.at[0, rows_of(c)],
            packets_in.at[k, rows_of(c)],
            packet_send.at[0, c],
            packet_recv.at[k, c],
            (my_y, lax.rem(my_x + 1, n_gx)),
        )

    def guarded(condition, act):
        if condition is None:
            act()
        else:
            pl.when(condition)(act)

    def send_own(t, carry):
        for condition, copy in own_copies((t + chunks - 1) % chunks):
            guarded(condition, copy.start)
        return carry

    for p in range(8):
        mine[pl.ds(p, 1)] = jnp.full((1, LANES), columns[min(p, bricks - 1)], jnp.int32)
    if layered:
        copies = [
            to_peer(step, mine, table.at[my_x], table_send, table_recv) for step in range(1, n_gx)
        ]
        for copy in copies:
            copy.start()
        keep = pltpu.make_async_copy(second, cols.at[z], own_sem)
        pl.when(inner)(keep.start)
    lax.fori_loop(0, AHEAD, send_own, 0)
    for l in range(LEVELS):
        u, w, wq, h = iterates[l], ws[l], wqs[l], hs[l]
        for b in range(BUFFERS[l]):
            zero_row = jnp.zeros((3, wq + 2 * PAD, LANES), jnp.float32)
            u[b, :, 0] = zero_row
            u[b, :, h + 1] = zero_row
            halos[l][b] = jnp.zeros(halos[l].shape[1:], jnp.float32)
    iterates[LEVELS - 1][...] = jnp.zeros(iterates[LEVELS - 1].shape, jnp.float32)

    def wanted(entry):
        value = entry(0)
        for p in range(1, bricks):
            value = jnp.where(group == p, entry(p), value)
        return value

    picks[pl.ds(3, 1)] = wanted(lambda p: mine[pl.ds(p, 1)])
    if layered:
        pl.when(inner)(keep.wait)
        for copy in copies:
            copy.wait()
        for i, device in enumerate((2 * end, 2 * end + 1, 2 * z + 1 - x)):
            picks[pl.ds(i, 1)] = wanted(lambda p: table[device, pl.ds(p, 1)])

    def pick_of(i):
        return jnp.broadcast_to(picks[pl.ds(i, 1)], (across, LANES))

    def by_layer(values, layers):
        value = values[0]
        for k in range(1, LAYERS):
            value = jnp.where(layers == k, values[k], value)
        return value

    def forward(c):
        for k in range(LAYERS):

            @pl.when(z != k)
            def _(k=k):
                column_arrival(k, c).wait_recv()

        layers = [pick_of(i) // 2 for i in range(3)]
        for row in range(ROWS):
            r = c * ROWS + row
            values = [cols[k, r] for k in range(LAYERS)]
            for i in range(3):
                packets_out[i, r] = by_layer(values, layers[i])
        for copy in packet_copies(c)[::-1]:
            copy.start()

    def edges(c):
        return [
            (
                has_left,
                remote(avg_stage.at[c, 0], avg_halo.at[c, 1], edge_send.at[0, c], edge_recv.at[0, c], left),
                remote(avg_stage.at[c, 1], avg_halo.at[c, 0], edge_send.at[1, c], edge_recv.at[1, c], right),
            ),
            (
                has_right,
                remote(avg_stage.at[c, 1], avg_halo.at[c, 0], edge_send.at[1, c], edge_recv.at[1, c], right),
                remote(avg_stage.at[c, 0], avg_halo.at[c, 1], edge_send.at[0, c], edge_recv.at[0, c], left),
            ),
        ]

    def average(c, row, value):
        r = c * ROWS + row
        value = 0.5 * (first[r] + value)
        avg[r + 1, pl.ds(PAD, across)] = value
        avg_stage[c, 0, pl.ds(row, 1)] = value[0:1]
        avg_stage[c, 1, pl.ds(row, 1)] = value[across - 1 : across]

    def averages(c):
        pick = pick_of(3)
        if not layered:
            for step in range(1, n_gx):
                remote(
                    second.at[rows_of(c)],
                    cols.at[lax.rem(my_x - step + n_gx, n_gx), rows_of(c)],
                    own_send.at[step, c],
                    col_recv.at[step, c],
                    (my_y, lax.rem(my_x + step, n_gx)),
                ).wait_recv()
            for row in range(ROWS):
                value = second[c * ROWS + row]
                for step in range(1, n_gx):
                    k = lax.rem(my_x + step, n_gx)
                    value = jnp.where(pick == k, cols[k, c * ROWS + row], value)
                average(c, row, value)
        else:
            layer, side = pick // 2, pick % 2

            @pl.when(inner)
            def _():
                packet_arrival(1 - x, c).wait_recv()
                for row in range(ROWS):
                    r = c * ROWS + row
                    value = by_layer([cols[k, r] for k in range(LAYERS)], layer)
                    average(c, row, jnp.where(side == x, value, packets_in[1 - x, r]))

            @pl.when(ending)
            def _():
                column_arrival(z, c).wait_recv()
                for k in range(2):
                    packet_arrival(k, c).wait_recv()
                for row in range(ROWS):
                    r = c * ROWS + row
                    value = jnp.where(side == 0, packets_in[0, r], packets_in[1, r])
                    same = jnp.where(side == x, second[r], cols[z, r])
                    average(c, row, jnp.where(layer == z, same, value))

        for present, copy, _ in edges(c):
            pl.when(present)(copy.start)

    def place_average(c):
        for present, _, opposite in edges(c):
            pl.when(present)(opposite.wait_recv)
        for row in range(ROWS):
            r = c * ROWS + row
            avg[r + 1, pl.ds(PAD - 1, 1)] = avg_halo[c, 0, pl.ds(row, 1)]
            avg[r + 1, pl.ds(PAD + across, 1)] = avg_halo[c, 1, pl.ds(row, 1)]

    to_up = remote(avg.at[1], avg.at[height + 1], avg_send.at[0], avg_recv.at[0], up)
    to_down = remote(avg.at[height], avg.at[0], avg_send.at[1], avg_recv.at[1], down)
    row_parts = [(has_up, to_up, to_down), (has_down, to_down, to_up)]

    def row_flags(l, r):
        h = hs[l]
        at = my_y * h + r
        return flag(at > 0), flag(at < n_gy * h - 1)

    def masks_of(l):
        w, planes = ws[l], LANES >> l
        first_column = ones((sub > 0) | has_left)
        last_column = ones((sub != (w - 1) % 8) | has_right)
        below = ones((lane > 0) & (lane < planes))
        above = ones(lane < planes - 1)
        return first_column, last_column, below, above

    masks = [masks_of(l) for l in range(LEVELS)]

    def exchange(l, b):
        h, wq = hs[l], wqs[l]
        u, stage, halo = iterates[l], stages[l], halos[l]
        base = bases[l] + 4 * b
        inner = pl.ds(PAD, wq)
        send = [halo_send.at[base + d] for d in range(4)]
        recv = [halo_recv.at[base + d] for d in range(4)]
        to_up = remote(u.at[b, :, 1, inner], u.at[b, :, h + 1, inner], send[0], recv[0], up)
        to_down = remote(u.at[b, :, h, inner], u.at[b, :, 0, inner], send[1], recv[1], down)
        to_left = remote(stage.at[b, 0], halo.at[b, 1], send[2], recv[2], left)
        to_right = remote(stage.at[b, 1], halo.at[b, 0], send[3], recv[3], right)
        return [
            (has_up, to_up, to_down),
            (has_down, to_down, to_up),
            (has_left, to_left, to_right),
            (has_right, to_right, to_left),
        ]

    def place_halo(l, b, r):
        u, halo, w = iterates[l], halos[l], ws[l]
        for i in range(3):
            u[b, i, r + 1, pl.ds(PAD - 1, 1)] = halo[b, 0, i, pl.ds(r, 1)]
            u[b, i, r + 1, pl.ds(PAD + w, 1)] = halo[b, 1, i, pl.ds(r, 1)]

    def store_chunk(l, b, r, j, new):
        u, stage, w = iterates[l], stages[l], ws[l]
        for i in range(3):
            u[b, i, r + 1, pl.ds(PAD + 8 * j, 8)] = new[i]
            if j == 0:
                stage[b, 0, i, pl.ds(r, 1)] = new[i][0:1]
            if j == wqs[l] // 8 - 1:
                k = (w - 1) % 8
                stage[b, 1, i, pl.ds(r, 1)] = new[i][k : k + 1]

    last_sub = sub == 7

    def sweep(l, b, start, count, js, group, compute, store):
        u = iterates[l]
        first_column, last_column, below, above = masks[l]
        end = wqs[l] // 8 - 1
        scale = 0.25**l / (CONTRAST * CONTRAST) / (4.0 if l == 0 else 1.0)

        def at(r, j, shift=0):
            return [u[b, i, r + 1, pl.ds(PAD + 8 * j + shift, 8)] for i in range(3)]

        def face(before, after, mask):
            change = [q - p for p, q in zip(before, after)]
            spread = change[0] * change[0] + change[1] * change[1] + change[2] * change[2]
            if scale != 1.0:
                spread = spread * scale
            weight = lax.rsqrt(1.0 + spread)
            if mask is not None:
                weight = weight * mask
            return [weight * c for c in change] + [weight]

        def row(r, carry):
            flags = row_flags(l, r)
            results, lower, previous = [], [], None
            for n, j in enumerate(js):
                center = at(r, j)
                down = face(center, at(r + 1, j), flags[1])
                lower.append(down)
                side = face(center, [pltpu.roll(c, LANES - 1, 1) for c in center], above)
                right = face(center, at(r, j, 1), last_column if j == end else None)
                if j - 1 in js:
                    left = [
                        pltpu.roll(jnp.where(last_sub, p, q), 1, 0) for p, q in zip(previous, right)
                    ]
                else:
                    left = face(at(r, j, -1), center, first_column if j == 0 else None)
                previous = right
                back = face([pltpu.roll(c, 1, 1) for c in center], center, below)
                up = carry[n]
                flux = [
                    (down[i] - up[i]) + (side[i] - back[i]) + (right[i] - left[i]) for i in range(3)
                ]
                total = (down[3] + up[3]) + (side[3] + back[3]) + (right[3] + left[3])
                results.append(compute(r, j, center, flux, total))
            return results, lower

        def step(k, carry):
            base = start + k * group
            if 0 in js or end in js:
                for n in range(group):
                    place_halo(l, b, base + n)
            done = []
            for n in range(group):
                results, carry = row(base + n, carry)
                done.append(results)
            for n in range(group):
                for j, result in zip(js, done[n]):
                    store(base + n, j, result)
            return carry

        flags = row_flags(l, start)
        carry = [face(at(start - 1, j), at(start, j), flags[0]) for j in js]
        if count == group:
            step(0, carry)
        else:
            lax.fori_loop(0, count // group, step, carry)

    def part(l, b, which, compute, store):
        h = hs[l]
        every = tuple(range(wqs[l] // 8))
        if which == "all":
            sweep(l, b, 0, h, every, min(h, max(1, CELLS // len(every))), compute, store)
        elif which == "edge":
            sweep(l, b, 0, h, (every[0], every[-1]), CELLS, compute, store)
            for r in (0, h - 1):
                sweep(l, b, r, 1, every[1:-1], 1, compute, store)
        else:
            sweep(l, b, 1, h - 2, every[1:-1], 10, compute, store)

    def motion_of(r, j):
        return [moved[k, r, pl.ds(8 * j, 8)] for k in range(5)]

    def tensor_of(l, r, j):
        return [tensors[l][k, r, pl.ds(8 * j, 8)] for k in range(6)]

    def source_of(l, r, j):
        return [sources[l][k, r, pl.ds(8 * j, 8)] for k in range(3)]

    def relax(l, b, target, which="all"):
        coupling = 0.25**l
        gain = 0.5 if target is None else 1.0

        def compute(r, j, center, flux, total):
            if l == 0:
                h0, h1, h2, time, hh = motion_of(r, j)
                around = [q + total * c for q, c in zip(flux, center)]
                diagonal = TIKHONOV + total
                widened = diagonal + hh
                common = h0 * around[0] + h1 * around[1] + h2 * around[2] + diagonal * time
                inverse = (gain * RELAXATION) / (diagonal * widened)
                keep = gain * (1.0 - RELAXATION)
                return [
                    keep * c + (q * widened - g * common) * inverse
                    for c, q, g in zip(center, around, (h0, h1, h2))
                ]
            solved = solve_three(
                tensor_of(l, r, j),
                TIKHONOV + coupling * total,
                [
                    f + coupling * (q + total * c)
                    for f, q, c in zip(source_of(l, r, j), flux, center)
                ],
            )
            return [c + RELAXATION * (s - c) for c, s in zip(center, solved)]

        def store(r, j, new):
            if target is None:
                for i in range(3):
                    out[i, r, pl.ds(8 * j, 8)] = new[i]
            else:
                store_chunk(l, target, r, j, new)

        part(l, b, which, compute, store)

    def residue(l, b, which="all"):
        coupling = 0.25**l

        def compute(r, j, center, flux, total):
            if l == 0:
                h0, h1, h2, time, _ = motion_of(r, j)
                common = h0 * center[0] + h1 * center[1] + h2 * center[2] + time
                return [
                    q - TIKHONOV * c - g * common for c, q, g in zip(center, flux, (h0, h1, h2))
                ]
            value = apply_three(tensor_of(l, r, j), center)
            return [
                f + coupling * q - TIKHONOV * c - a
                for f, q, c, a in zip(source_of(l, r, j), flux, center, value)
            ]

        def store(r, j, new):
            for i in range(3):
                residues[l][i, r, pl.ds(8 * j, 8)] = new[i]

        part(l, b, which, compute, store)

    def enter(l):
        coupling = 0.25**l

        def compute(r, j, center, flux, total):
            tensor, given = tensor_of(l, r, j), source_of(l, r, j)
            value = apply_three(tensor, center)
            source = [
                f + a + TIKHONOV * c - coupling * q
                for f, a, c, q in zip(given, value, center, flux)
            ]
            solved = solve_three(tensor, TIKHONOV + coupling * total, given)
            return source, [c + RELAXATION * s for c, s in zip(center, solved)]

        def store(r, j, result):
            source, new = result
            for i in range(3):
                sources[l][i, r, pl.ds(8 * j, 8)] = source[i]
            store_chunk(l, 1, r, j, new)

        part(l, 0, "all", compute, store)

    fine_lane = lax.broadcasted_iota(jnp.int32, (LANES, LANES), 0)
    coarse_lane = lax.broadcasted_iota(jnp.int32, (LANES, LANES), 1)
    halving = ones(fine_lane // 2 == coarse_lane)
    squeeze = jnp.concatenate([halving, halving], axis=0).astype(jnp.bfloat16)
    doubling = ones(coarse_lane // 2 == fine_lane)
    spread = jnp.concatenate([doubling, doubling], axis=0).astype(jnp.bfloat16)

    def corners(j, k, rest):
        return [
            (row, pl.ds(rest + 16 * j + parity, k, stride=2)) for row in range(2) for parity in range(2)
        ]

    def filled(x):
        if x.shape[0] == 8:
            return x
        return jnp.concatenate([x, jnp.zeros((8 - x.shape[0], LANES), jnp.float32)], axis=0)

    def shrink(l, rows, sums, factor, store):
        chunks = wqs[l + 1] // 8
        pieces = [[sums(r, j) for j in range(chunks)] for r in rows]
        flat = [filled(x) for of_row in pieces for of_chunk in of_row for x in of_chunk]
        y = dot(two_terms(jnp.concatenate(flat, axis=0), 1), squeeze) * factor
        at = 0
        for r in rows:
            for j in range(chunks):
                for i in range(len(pieces[0][0])):
                    store(r, j, i, y[8 * at : 8 * at + 8])
                    at += 1

    def summed(load, cells):
        values = [load(row, columns) for row, columns in cells]
        return (values[0] + values[1]) + (values[2] + values[3])

    def all_rows(l, work):
        group = min(4, hs[l])

        def step(k, carry):
            work([k * group + n for n in range(group)])
            return carry

        if hs[l] == group:
            step(0, 0)
        else:
            lax.fori_loop(0, hs[l] // group, step, 0)

    def shrink_iterate(l, b):
        u = iterates[l]
        coarse, stage, w = iterates[l + 1], stages[l + 1], ws[l + 1]
        k = min(8, w)

        def sums(r, j):
            cells = corners(j, k, PAD)
            return [
                summed(lambda row, columns, i=i: u[b, i, 2 * r + row + 1, columns], cells)
                for i in range(3)
            ]

        def store(r, j, i, y):
            coarse[0, i, r + 1, pl.ds(PAD + 8 * j, 8)] = y
            if j == 0:
                stage[0, 0, i, pl.ds(r, 1)] = y[0:1]
            if j == wqs[l + 1] // 8 - 1:
                n = (w - 1) % 8
                stage[0, 1, i, pl.ds(r, 1)] = y[n : n + 1]

        factor = 0.0625 if l == 0 else 0.125
        all_rows(l + 1, lambda rows: shrink(l, rows, sums, factor, store))

    def shrink_array(l, fine, coarse, factor):
        k = min(8, ws[l + 1])

        def sums(r, j):
            cells = corners(j, k, 0)
            return [
                summed(lambda row, columns, i=i: fine[i, 2 * r + row, columns], cells)
                for i in range(fine.shape[0])
            ]

        def store(r, j, i, y):
            coarse[i, r, pl.ds(8 * j, 8)] = y

        all_rows(l + 1, lambda rows: shrink(l, rows, sums, factor, store))

    def shrink_motion(rows):
        def sums(r, j):
            values = None
            for row, columns in corners(j, min(8, ws[1]), 0):
                h0, h1, h2 = [moved[k, 2 * r + row, columns] for k in range(3)]
                terms = [h0 * h0, h0 * h1, h0 * h2, h1 * h1, h1 * h2, h2 * h2]
                values = terms if values is None else [v + t for v, t in zip(values, terms)]
            return values

        def store(r, j, i, y):
            tensors[1][i, r, pl.ds(8 * j, 8)] = y

        shrink(0, rows, sums, 0.125, store)

    def grow(l, b, solved, target, arriving):
        wc, hc, h = wqs[l + 1], hs[l + 1], hs[l]
        kc, kr = min(8, ws[l + 1]), min(8, hc)
        u, coarse = iterates[l], iterates[l + 1]

        def spread_out(x):
            y = dot(two_terms(x, 1), spread)
            return 2.0 * y if l == 0 else y

        def correction(r):
            inner = pl.ds(PAD, wc)
            return (coarse[solved, :, r + 1, inner] - coarse[0, :, r + 1, inner]).reshape(3 * wc, LANES)

        def add(y, first_row, targets):
            for i in range(3):
                for j in range(wc // 8):
                    at = first_row + i * wc + 8 * j
                    piece = y[at : at + kc]
                    for row in targets:
                        for parity in range(2):
                            columns = pl.ds(PAD + 16 * j + parity, kc, stride=2)
                            u[target, i, row, columns] = u[b, i, row, columns] + piece

        def work(rows):
            y = spread_out(jnp.concatenate([correction(r) for r in rows], axis=0))
            for n, r in enumerate(rows):
                add(y, n * 3 * wc, (2 * r + 1, 2 * r + 2))

        all_rows(l + 1, work)
        wait_all(arriving)
        y = spread_out(jnp.concatenate([correction(-1), correction(hc)], axis=0))
        add(y, 0, (0,))
        add(y, 3 * wc, (h + 1,))
        hq = max(8, hc)
        halo, coarse_halo = halos[l], halos[l + 1]
        y = spread_out((coarse_halo[solved] - coarse_halo[0]).reshape(6 * hq, LANES))
        for side in range(2):
            for i in range(3):
                for j in range(hq // 8):
                    at = (side * 3 + i) * hq + 8 * j
                    for parity in range(2):
                        rows = pl.ds(16 * j + parity, kr, stride=2)
                        halo[target, side, i, rows] = halo[b, side, i, rows] + y[at : at + kr]

    first_column, last_column, below, above = masks[0]

    def motion(r):
        flags = row_flags(0, r)
        for j in range(across // 8):
            s = PAD + 8 * j
            diffs, sums = [], []
            for shift in (-1, 0, 1):
                lower = avg[r, pl.ds(s + shift, 8)]
                middle = avg[r + 1, pl.ds(s + shift, 8)]
                upper = avg[r + 2, pl.ds(s + shift, 8)]
                diffs.append(0.5 * (upper - lower))
                sums.append(0.25 * (lower + 2.0 * middle + upper))
            along_rows = 0.25 * (diffs[0] + 2.0 * diffs[1] + diffs[2])
            along_cols = 0.5 * (sums[2] - sums[0])
            along_planes = 0.25 * (sums[0] + 2.0 * sums[1] + sums[2])

            def beside(x):
                return pltpu.roll(x, 1, 1) * below, pltpu.roll(x, LANES - 1, 1) * above

            def smooth(x):
                lower, upper = beside(x)
                return 0.25 * (lower + 2.0 * x + upper)

            g0, g1 = smooth(along_rows), smooth(along_cols)
            lower, upper = beside(along_planes)
            g2 = 0.5 * (upper - lower)
            square = g0 * g0 + g1 * g1 + g2 * g2
            root = lax.rsqrt(square + FLOOR)
            h = [g0 * root, g1 * root, g2 * root]
            hh = square * root * root
            base = first[r, pl.ds(8 * j, 8)]
            time = (4.0 * root) * (avg[r + 1, pl.ds(s, 8)] - base)
            for k, value in enumerate((*h, time, hh)):
                moved[k, r, pl.ds(8 * j, 8)] = value
            total = below + above + (flags[0] + flags[1])
            total = total + (first_column if j == 0 else 1.0)
            total = total + (last_column if j == across // 8 - 1 else 1.0)
            length = time * (-RELAXATION / (TIKHONOV + total + hh))
            store_chunk(0, 0, r, j, [g * length for g in h])

    def shrink_block(m):
        shrink_motion([m * (ROWS // 2) + k for k in range(ROWS // 2)])

    def motion_block(m):
        for row in range(ROWS):
            motion(m * ROWS + row)
        shrink_block(m)

    def gather_step(s, carry):
        @pl.when(s + AHEAD < chunks)
        def _():
            send_own(s + AHEAD, 0)

        def chunk_at(t):
            return (t + chunks - 1) % chunks

        if layered:
            pl.when(inner & (s < chunks))(lambda: forward(chunk_at(s)))
        pl.when((s >= 1) & (s <= chunks))(lambda: averages(chunk_at(s - 1)))
        pl.when(s >= 2)(lambda: place_average(chunk_at(s - 2)))
        pl.when(s == 3)(lambda: start_all(row_parts))
        pl.when(s >= 5)(lambda: motion_block(s - 4))

        @pl.when(s == chunks)
        def _():
            wait_all(row_parts)
            motion_block(0)
            for row in range(1, ROWS):
                motion(height - ROWS + row)

        return carry

    lax.fori_loop(0, chunks + 2, gather_step, 0)
    for row in range(ROWS):
        motion((chunks - 2) * ROWS + row)
    motion(height - ROWS)
    arriving = exchange(0, 0)
    start_all(arriving)
    shrink_block(chunks - 2)
    shrink_block(chunks - 1)

    def finish_sends(c, carry):
        for condition, copy in own_copies(c):
            guarded(condition, copy.wait_send)
        if layered:
            for copy in packet_copies(c):
                pl.when(inner)(copy.wait_send)
        for present, copy, _ in edges(c):
            pl.when(present)(copy.wait_send)
        return carry

    lax.fori_loop(0, chunks, finish_sends, 0)
    for l in range(1, LEVELS - 1):
        shrink_array(l, tensors[l], tensors[l + 1], 0.125)
    relax(0, 0, 1, "inner")
    wait_all(arriving)
    relax(0, 0, 1, "edge")
    for l in range(LEVELS - 1):
        b = 1 if l == 0 else 2
        current = exchange(l, b)
        start_all(current)
        shrink_iterate(l, b)
        following = exchange(l + 1, 0)
        start_all(following)
        if l == 0:
            residue(l, b, "inner")
        wait_all(current)
        residue(l, b, "edge" if l == 0 else "all")
        shrink_array(l, residues[l], sources[l + 1], 0.0625 if l == 0 else 0.125)
        wait_all(following)
        enter(l + 1)
        current = exchange(l + 1, 1)
        start_all(current)
        wait_all(current)
        relax(l + 1, 1, 2)
    for l in range(LEVELS - 2, -1, -1):
        b = 1 if l == 0 else 2
        solved = 2 if l == LEVELS - 2 else 5
        arriving = exchange(l + 1, solved)
        start_all(arriving)
        grow(l, b, solved, b + 1, arriving)
        if l > 0:
            relax(l, b + 1, b + 2)
            current = exchange(l, b + 2)
            start_all(current)
            wait_all(current)
            relax(l, b + 2, b + 3)
    relax(0, 2, 3, "edge")
    current = exchange(0, 3)
    start_all(current)
    relax(0, 2, 3, "inner")
    relax(0, 3, None, "inner")
    wait_all(current)
    relax(0, 3, None, "edge")


def body(n_gy, n_gx, first_frame, second_frame, source_column):
    height, across, planes = first_frame.shape
    f32 = jnp.float32
    hs = [height >> l for l in range(LEVELS)]
    wqs = [max(across >> l, 8) for l in range(LEVELS)]
    hqs = [max(h, 8) for h in hs]
    total = sum(BUFFERS) * 4
    vmem = pl.BlockSpec(memory_space=pltpu.VMEM)
    chunks = height // ROWS
    layered = n_gx == 2 * LAYERS
    volume = (height, across, LANES)
    scratch = [
        pltpu.VMEM((LAYERS if layered else n_gx, *volume), f32),
        pltpu.VMEM((2, *volume) if layered else (2, 8, LANES), f32),
        pltpu.VMEM((3, *volume) if layered else (3, 8, LANES), f32),
        pltpu.VMEM((height + 2, across + 2 * PAD, LANES), f32),
        pltpu.VMEM((chunks, 2, 8, LANES), f32),
        pltpu.VMEM((chunks, 2, 8, LANES), f32),
    ]
    scratch += [pltpu.VMEM((6 if l else 5, hs[l], wqs[l], LANES), f32) for l in range(LEVELS)]
    scratch += [pltpu.VMEM((3, hs[l], wqs[l], LANES), f32) for l in range(1, LEVELS)]
    scratch += [
        pltpu.VMEM((BUFFERS[l], 3, hs[l] + 2, wqs[l] + 2 * PAD, LANES), f32)
        for l in range(LEVELS)
    ]
    scratch += [pltpu.VMEM((BUFFERS[l], 2, 3, hqs[l], LANES), f32) for l in range(LEVELS)] * 2
    scratch += [pltpu.VMEM((3, hs[l], wqs[l], LANES), f32) for l in range(LEVELS - 1)]
    dma = pltpu.SemaphoreType.DMA
    scratch += [dma((total,)), dma((total,)), dma((2,)), dma((2,)), dma]
    scratch += [
        pltpu.VMEM((8, LANES), jnp.int32),
        pltpu.VMEM((n_gx, 8, LANES), jnp.int32),
        pltpu.VMEM((8, LANES), jnp.int32),
        dma((n_gx,)),
        dma((n_gx,)),
        dma((3 if layered else n_gx, chunks)),
        dma((3, chunks)),
        dma((LAYERS if layered else n_gx, chunks)),
        dma((2, chunks)),
        dma((2, chunks)),
        dma((2, chunks)),
        dma((3,)),
        pltpu.VMEM(volume, f32),
        pltpu.VMEM(volume, f32),
        pltpu.SMEM((source_column.size,), jnp.int32),
    ]
    columns = source_column.reshape(-1)
    return pl.pallas_call(
        functools.partial(kernel, n_gy, n_gx, height, across),
        out_shape=jax.ShapeDtypeStruct((3, height, across, planes), f32),
        in_specs=[pl.BlockSpec(memory_space=pltpu.HBM)] * 3,
        out_specs=vmem,
        scratch_shapes=scratch,
        compiler_params=pltpu.CompilerParams(
            collective_id=0, has_side_effects=True, vmem_limit_bytes=40 * 1024 * 1024
        ),
    )(*(pltpu.with_memory_space_constraint(x, pltpu.HBM) for x in (first_frame, second_frame, columns)))


def solution(mesh):
    return jax.shard_map(
        functools.partial(body, mesh.shape["gy"], mesh.shape["gx"]),
        mesh=mesh,
        in_specs=(P("gy", "gx", None), P("gy", "gx", None), P("gy", "gx", None, None)),
        out_specs=P(None, "gy", "gx", None),
        check_vma=False,
    )
```
